128 devices in a mesh: sgt: 8 (over z, core), work: 16 (over y, x).
Axes of the slice: x: 4, y: 4, z: 4, core: 2. Of those that a mesh axis runs over, the one named last changes fastest.
Arguments:
- sgt_tensor: bfloat16 [32, 6, 2, 128, 1024], P('sgt'), may hold values from -6 to 6
- moment: float32 [32, 6, 128], P('sgt'), may hold values from -2.5 to 2.5
- slip_rate: bfloat16 [128, 8, 64, 128, 32], P(('sgt', 'work')), may hold values from 0 to 0.011047363
- footprint: int32 [128, 8], replicated, may hold values from 0 to 31, as said below
- live_blocks: int32 [128], replicated, may hold values from 1 to 8
- start_delay: int32 [128, 8], replicated, may hold values from 0 to 255
- frequency: float32 [44], replicated, may hold values from 0.05 to 1.5
- period_owner: int32 [44], replicated, may hold values from 0 to 15, as said below
Outputs:
- spectral_peaks: float32 [16, 3, 2, 128, 64], P('work', None, None, 'sgt')
The draws below stay inside these ranges and needn't reach their ends.
Inputs may be any that keep to these rules, and one draw needn't show every extreme that they name: `footprint`: slot k of rupture r names block ((c + k) mod 8) * 4 + ((c + k) mod 32) // 8 for a strike column c of that rupture; so the slots of one rupture name blocks of distinct indices of sgt, block b being held by index b // 4. `period_owner`: each index of work owns 44 // 16 or 3 periods.
All inputs are finite; a program needn't handle non-finite values.
Results may differ from the reference program's by a relative error of at most 0.0024.
Values may be sent and summed in bfloat16 or wider, within the bound.
No kernel may reach another device: no remote copies, remote signals or barrier semaphores. Data moves between devices by JAX's collectives and lax.ppermute only.
A program may use at most 192 MiB of HBM per device.

```python
import math
import jax
import jax.numpy as jnp
from jax import lax

NT = 1024
NCOMP = 2
NJ = 6
PB = 128
L = 32
OFFMAX = 256
KIR = 512
NPER = 44
V = 64
BLK_SGT = 4
NB = 32
R = 128
FMAX = 8
PMAX = 3
N_WORK = 16


def draw_footprint(key, part):
    column_start = jax.random.randint(key, (R, 1), 0, NB)
    column = (column_start + jnp.arange(FMAX)[None, :]) % NB
    return (column % FMAX * BLK_SGT + column // FMAX).astype(jnp.int32)


def draw_start_delay(key, part):
    values = jax.random.randint(key, (R, FMAX), 0, OFFMAX)
    return values.at[0, 0].set(OFFMAX - 1).astype(jnp.int32)


def draw_period_owner(key, part):
    order = jax.random.permutation(key, NPER)
    placing = jnp.argsort(order, stable=True)
    return (placing % N_WORK).astype(jnp.int32)


def touch_ends(result, own_key, low, largest):
    longest = result.shape.index(max(result.shape))
    spots = []
    for shift in (0, 1):
        where = [jax.random.randint(jax.random.fold_in(own_key, axis), (), 0, length) for axis, length in enumerate(result.shape)]
        where[longest] = (where[longest] + shift) % result.shape[longest]
        spots.append(tuple(where))
    return result.at[spots[0]].set(low).at[spots[1]].set(largest)


def steps_of(stream_key, dims, split, smallest, top_value):
    def one(axis_at, blocks):
        draws = jax.random.uniform(jax.random.fold_in(jax.random.fold_in(stream_key, 6), axis_at), (blocks,), jnp.float32, smallest / len(split), top_value / len(split))
        return jnp.repeat(jnp.exp(draws), dims[axis_at] // blocks).reshape((-1,) + (1,) * (len(dims) - axis_at - 1))

    factor_of = one(*split[0])
    for cut in split[1:]:
        factor_of = factor_of * one(*cut)
    return factor_of


def centred(rng, shape, scale, limit, pieces=(), kind=jnp.bfloat16):
    values = jax.random.normal(rng, shape, jnp.float32) * scale
    if len(pieces) > 0:
        values = steps_of(rng, shape, pieces, -0.22, 0.18) * values
    return jnp.clip(values, min=-limit, max=limit).astype(kind)


def setup_inputs(seed: int = 0) -> dict:
    streams_of = jax.random.split(jax.random.key(seed), 9)
    sgt_tensor = centred(streams_of[0], (NB, NJ, NCOMP, PB, NT), 1.0, 6.0, ((0, 8),))
    moment = centred(streams_of[1], (NB, NJ, PB), 0.4, 2.5, ((0, 8),), jnp.float32)
    slip_rate = jnp.clip(0.011047363 * jax.random.uniform(streams_of[2], (R, FMAX, V, PB, L), jnp.float32) ** steps_of(streams_of[2], (R, FMAX, V, PB, L), ((0, 128),), -0.2, 0.2), 0.0, 0.011047363).astype(jnp.bfloat16)
    footprint = draw_footprint(jax.random.fold_in(streams_of[8], 71), 0)
    live_blocks = touch_ends(jax.random.randint(streams_of[4], (R,), 1, FMAX + 1), jax.random.fold_in(streams_of[4], 1), 1, FMAX).astype(jnp.int32)
    start_delay = draw_start_delay(jax.random.fold_in(streams_of[8], 71), 0)
    frequency = jnp.clip(jnp.exp(jax.random.uniform(streams_of[6], (NPER,), jnp.float32, math.log(0.05), math.log(1.5))), 0.05, 1.5)
    period_owner = draw_period_owner(jax.random.fold_in(streams_of[8], 71), 0)
    return {"sgt_tensor": sgt_tensor, "moment": moment, "slip_rate": slip_rate, "footprint": footprint, "live_blocks": live_blocks, "start_delay": start_delay, "frequency": frequency, "period_owner": period_owner}


damping = 0.05

def project_block(bundle):
    tensor_block, weights = bundle
    summed = lax.optimization_barrier(jnp.sum(weights[:, None, :, None] * tensor_block.astype(jnp.float32), axis=0))
    return summed.astype(jnp.bfloat16)

def hankel(shifted, width, steps):
    length = shifted.shape[-1]
    leading = shifted.shape[:-1]
    repeated = jnp.broadcast_to(shifted[..., None, :], leading + (width, length))
    flattened = repeated.reshape(leading + (width * length,))
    flattened = jnp.concatenate([flattened, jnp.zeros(leading + (width,), shifted.dtype)], axis=-1)
    return flattened.reshape(leading + (width, length + 1))[..., :steps]

def convolve(tensor_block, slip_window, delay):
    channels, points, samples = tensor_block.shape
    padding = jnp.zeros((channels, points, OFFMAX + L - 1), tensor_block.dtype)
    ending = jnp.zeros((channels, points, 1), tensor_block.dtype)
    extended = jnp.concatenate([padding, tensor_block, ending], axis=2)
    begin = (OFFMAX - delay).astype(jnp.int32)
    shifted = lax.dynamic_slice_in_dim(extended, begin, samples + L, axis=2)
    windows = hankel(shifted, L, samples)
    reversed_slip = slip_window[:, :, ::-1]
    return jnp.einsum('viq,ciqt->vct', reversed_slip.astype(jnp.float32), windows.astype(jnp.float32))

def response_matrix(angular):
    delays = jnp.arange(NT)[None, :] - jnp.arange(NT)[:, None]
    elapsed = jnp.maximum(delays, 0).astype(jnp.float32)
    damped = angular * math.sqrt(1.0 - damping * damping)
    kernel = angular * angular * jnp.exp(-damping * angular * elapsed) * jnp.sin(damped * elapsed) / damped
    inside = (delays >= 0) & (delays < KIR)
    return jnp.where(inside, kernel, jnp.zeros_like(kernel)).astype(jnp.bfloat16)

def reference(sgt_tensor, moment, slip_rate, footprint, live_blocks, start_delay, frequency, period_owner):
    projected = lax.map(project_block, (sgt_tensor, moment))

    def one_rupture(bundle):
        slips, blocks, live_count, delays = bundle

        def add_slot(slot_index, running):
            position = jnp.asarray(slot_index).astype(jnp.int32)
            block_id = blocks[position].astype(jnp.int32)
            tensor_block = lax.dynamic_index_in_dim(projected, block_id, 0, keepdims=False)
            slip_window = lax.dynamic_index_in_dim(slips, position, 0, keepdims=False)
            term = convolve(tensor_block, slip_window, delays[position])
            return running + jnp.where(position < live_count, term, jnp.zeros_like(term))
        running = lax.fori_loop(0, FMAX, add_slot, jnp.zeros((V, NCOMP, NT), jnp.float32))
        return running.astype(jnp.bfloat16)
    traces = lax.map(one_rupture, (slip_rate, footprint, live_blocks, start_delay))
    trace_rows = traces.reshape(R * V * NCOMP, NT)

    def peak(angular):
        motion = jnp.dot(trace_rows, response_matrix(angular), preferred_element_type=jnp.float32)
        return lax.optimization_barrier(jnp.max(jnp.abs(motion), axis=1)).reshape(R, V, NCOMP)
    peak_values = lax.map(peak, frequency)
    ordered = jnp.transpose(peak_values, (0, 3, 1, 2))
    period_ids = jnp.arange(NPER)
    same_owner = period_owner[:, None] == period_owner[None, :]
    earlier = period_ids[None, :] < period_ids[:, None]
    period_rank = lax.optimization_barrier(jnp.sum(same_owner & earlier, axis=1))

    def one_owner(owner_index):
        chosen = (period_owner[None, :] == owner_index) & (period_rank[None, :] == jnp.arange(PMAX)[:, None])
        picked = jnp.where(chosen[:, :, None, None, None], ordered[None], jnp.zeros_like(ordered[None]))
        return lax.optimization_barrier(jnp.sum(picked, axis=1))
    return lax.map(one_owner, jnp.arange(N_WORK).astype(jnp.int32))
```

```python
import functools
import math

import jax
import jax.numpy as jnp
from jax import lax
from jax.experimental import pallas as pl
from jax.experimental.pallas import tpu as pltpu
from jax.sharding import PartitionSpec as P

NT = 1024
L = 32
KIR = 512
V = 64
PB = 128
NPER = 44
SLOTS = 8
HELD = 4
NJ = 6
PMAX = 3
OWNERS = 16
damping = 0.05

PHASES = 4
TAPS = 9
PADROWS = 16
BLOCK = 256
QSTEP = 4
VMEM = 60 * 1024 * 1024


def project_kernel(fp_ref, sgt_ref, mom_ref, out_ref, scr, sem):
    b = pl.program_id(0)
    me = lax.axis_index("sgt")
    work = lax.axis_index("work")
    weights = jnp.transpose(mom_ref[0])
    for c in range(2):
        for i in range(0, PB, 16):
            total = None
            for j in range(NJ):
                term = weights[i : i + 16, j : j + 1] * sgt_ref[0, j, c, i : i + 16, :].astype(
                    jnp.float32
                )
                total = term if total is None else total + term
            scr[b, c, i : i + 16, :] = total.astype(jnp.bfloat16)

    def wanted(g):
        base = (g * OWNERS + work) * SLOTS
        found = jnp.int32(0)
        for k in range(SLOTS):
            block = fp_ref[base + k]
            found = jnp.where(block // HELD == me, block % HELD, found)
        return found

    for g in range(SLOTS):
        copy = pltpu.make_async_copy(scr.at[b], out_ref.at[g], sem.at[g])
        pl.when(wanted(g) == b)(copy.start)

    @pl.when(b == HELD - 1)
    def _():
        for g in range(SLOTS):
            pltpu.make_async_copy(scr.at[0], out_ref.at[g], sem.at[g]).wait()


def project(footprint, sgt_tensor, moment):
    return pl.pallas_call(
        project_kernel,
        out_shape=jax.ShapeDtypeStruct((SLOTS, 2, PB, NT), jnp.bfloat16),
        grid_spec=pltpu.PrefetchScalarGridSpec(
            num_scalar_prefetch=1,
            grid=(HELD,),
            in_specs=[
                pl.BlockSpec((1, NJ, 2, PB, NT), lambda b, fp: (b, 0, 0, 0, 0)),
                pl.BlockSpec((1, NJ, PB), lambda b, fp: (b, 0, 0)),
            ],
            out_specs=pl.BlockSpec(memory_space=pl.ANY),
            scratch_shapes=[
                pltpu.VMEM((HELD, 2, PB, NT), jnp.bfloat16),
                pltpu.SemaphoreType.DMA((SLOTS,)),
            ],
        ),
        compiler_params=pltpu.CompilerParams(vmem_limit_bytes=VMEM),
        name="project",
    )(footprint, sgt_tensor, moment)


def tables_kernel(u_ref, v_ref, out_ref):
    columns = jnp.transpose(u_ref[0])
    row = lax.broadcasted_iota(jnp.int32, (BLOCK, BLOCK), 0)
    lane = lax.broadcasted_iota(jnp.int32, (BLOCK, BLOCK), 1)
    source = (lane % (BLOCK // PHASES)) * PHASES + lane // (BLOCK // PHASES)
    for n in range(QSTEP):
        sine = columns[:, 2 * n : 2 * n + 1]
        cosine = columns[:, 2 * n + 1 : 2 * n + 2]
        for j in range(3):
            span = slice(j * BLOCK, (j + 1) * BLOCK)
            value = sine * v_ref[0, 2 * n : 2 * n + 1, span] - (
                cosine * v_ref[0, 2 * n + 1 : 2 * n + 2, span]
            )
            if j == 0:
                value = jnp.where(row >= source, value, 0.0)
            if j == 2:
                value = jnp.where(row < source, value, 0.0)
            out_ref[n, :, span] = value.astype(jnp.bfloat16)


def tables(frequency):
    angular = frequency[:, None]
    damped = angular * math.sqrt(1.0 - damping * damping)
    rows = jnp.arange(BLOCK, dtype=jnp.float32)[None, :]
    decay = jnp.exp(-damping * angular * rows)
    u = jnp.stack([decay * jnp.sin(damped * rows), decay * jnp.cos(damped * rows)], axis=1)
    lane = jnp.arange(3 * BLOCK)
    inner = lane % BLOCK
    source = (inner % (BLOCK // PHASES)) * PHASES + inner // (BLOCK // PHASES)
    back = (source - (lane // BLOCK) * BLOCK).astype(jnp.float32)[None, :]
    growth = angular * angular / damped * jnp.exp(damping * angular * back)
    v = jnp.stack([growth * jnp.cos(damped * back), growth * jnp.sin(damped * back)], axis=1)
    steps = NPER // QSTEP
    return pl.pallas_call(
        tables_kernel,
        out_shape=jax.ShapeDtypeStruct((NPER, BLOCK, 3 * BLOCK), jnp.bfloat16),
        grid=(steps,),
        in_specs=[
            pl.BlockSpec((1, 2 * QSTEP, BLOCK), lambda s: (s, 0, 0)),
            pl.BlockSpec((1, 2 * QSTEP, 3 * BLOCK), lambda s: (s, 0, 0)),
        ],
        out_specs=pl.BlockSpec((QSTEP, BLOCK, 3 * BLOCK), lambda s: (s, 0, 0)),
        compiler_params=pltpu.CompilerParams(vmem_limit_bytes=VMEM),
        cost_estimate=pl.CostEstimate(
            flops=NPER * 3 * BLOCK * BLOCK * 5, bytes_accessed=20000000, transcendentals=0
        ),
        name="tables",
    )(u.reshape(steps, 2 * QSTEP, BLOCK), v.reshape(steps, 2 * QSTEP, 3 * BLOCK))


def gather_phases(delay, tensor_ref, phases):
    rows = lax.broadcasted_iota(jnp.int32, (BLOCK, 2 * BLOCK), 0)
    lane = lax.broadcasted_iota(jnp.int32, (BLOCK, 2 * BLOCK), 1)
    part = BLOCK // PHASES
    source = BLOCK + (rows % part) * PHASES + rows // part - delay
    pick = jnp.where(lane == source, 1.0, 0.0).astype(jnp.bfloat16)
    for a in range(NT // BLOCK):
        low = max(a - 1, 0) * BLOCK
        window = tensor_ref[:, low : (a + 1) * BLOCK]
        chosen = pick[:, 2 * BLOCK - window.shape[1] :]
        moved = lax.dot_general(
            chosen, window, (((1,), (1,)), ((), ())), preferred_element_type=jnp.float32
        )
        for c in range(2):
            for b in range(PHASES):
                phases[
                    c, PADROWS + a * part : PADROWS + (a + 1) * part, b * PB : (b + 1) * PB
                ] = moved[b * part : (b + 1) * part, c * PB : (c + 1) * PB]


def convolve_kernel(info_ref, tensor_ref, slip_ref, out_ref, phases, left, right, total):
    k = pl.program_id(0)

    @pl.when(k == 0)
    def _():
        total[...] = jnp.zeros_like(total)
        phases[:, :PADROWS, :] = jnp.zeros((2, PADROWS, PHASES * PB), jnp.float32)

    @pl.when(k < info_ref[0])
    def _():
        gather_phases(info_ref[1 + SLOTS + k], tensor_ref.at[0], phases)
        depth = PHASES * PB
        for j in range(TAPS):
            for c in range(2):
                left[c * BLOCK : (c + 1) * BLOCK, j * depth : (j + 1) * depth] = phases[
                    c, PADROWS - j : PADROWS - j + BLOCK, :
                ].astype(jnp.bfloat16)
            for b in range(PHASES):
                first = (PHASES * j - b + PHASES - b % 2) * V
                right[j * depth + b * PB : j * depth + (b + 1) * PB, :] = slip_ref[
                    0, b % 2, :, first : first + PHASES * V
                ]
        total[...] += jnp.dot(left[...], right[...], preferred_element_type=jnp.float32)

    @pl.when(k == SLOTS - 1)
    def _():
        part = BLOCK // PHASES
        lane = lax.broadcasted_iota(jnp.int32, (part, 2 * V), 1)
        for a in range(NT // BLOCK):
            for b in range(PHASES):
                half = slice((b // 2) * 2 * V, (b // 2 + 1) * 2 * V)
                first = total[a * part : (a + 1) * part, half]
                second = total[BLOCK + a * part : BLOCK + (a + 1) * part, half]
                if b % 2 == 0:
                    second = pltpu.roll(second, V, 1)
                else:
                    first = pltpu.roll(first, V, 1)
                out_ref[b * part : (b + 1) * part, a * 2 * V : (a + 1) * 2 * V] = jnp.where(
                    lane < V, first, second
                ).astype(jnp.bfloat16)


def convolve(info, incoming, slips):
    def live(k, info):
        return jnp.minimum(k, info[0] - 1)

    width = slips.shape[-1]
    return pl.pallas_call(
        convolve_kernel,
        out_shape=jax.ShapeDtypeStruct((BLOCK, NT // BLOCK * 2 * V), jnp.bfloat16),
        grid_spec=pltpu.PrefetchScalarGridSpec(
            num_scalar_prefetch=1,
            grid=(SLOTS,),
            in_specs=[
                pl.BlockSpec((1, 2 * PB, NT), lambda k, info: (info[1 + live(k, info)], 0, 0)),
                pl.BlockSpec((1, 2, PB, width), lambda k, info: (live(k, info), 0, 0, 0)),
            ],
            out_specs=pl.BlockSpec((BLOCK, NT // BLOCK * 2 * V), lambda k, info: (0, 0)),
            scratch_shapes=[
                pltpu.VMEM((2, PADROWS + BLOCK, PHASES * PB), jnp.float32),
                pltpu.VMEM((2 * BLOCK, TAPS * PHASES * PB), jnp.bfloat16),
                pltpu.VMEM((TAPS * PHASES * PB, PHASES * V), jnp.bfloat16),
                pltpu.VMEM((2 * BLOCK, PHASES * V), jnp.float32),
            ],
        ),
        compiler_params=pltpu.CompilerParams(vmem_limit_bytes=VMEM),
        name="convolve",
    )(info, incoming, slips)


def motion_kernel(place_ref, table_ref, trace_ref, out_ref, stacked):
    step = pl.program_id(0)
    width = NT // BLOCK * 2 * V

    @pl.when(step == 0)
    def _():
        out_ref[...] = jnp.zeros_like(out_ref)
        for j in range(3):
            shift = j * 2 * V
            rows = slice(j * BLOCK, (j + 1) * BLOCK)
            if j > 0:
                stacked[rows, :shift] = jnp.zeros((BLOCK, shift), jnp.bfloat16)
            stacked[rows, shift:] = trace_ref[:, : width - shift]

    for n in range(QSTEP):
        early = jnp.dot(
            table_ref[n, :, : 2 * BLOCK],
            stacked[: 2 * BLOCK, : width // 2],
            preferred_element_type=jnp.float32,
        )
        late = jnp.dot(
            table_ref[n], stacked[:, width // 2 :], preferred_element_type=jnp.float32
        )
        both = jnp.maximum(jnp.abs(early), jnp.abs(late))
        highest = jnp.max(both, axis=0, keepdims=True)
        highest = jnp.maximum(highest[:, : 2 * V], highest[:, 2 * V :])
        out_ref[pl.ds(place_ref[step * QSTEP + n], 1), :] = highest


def motion(place, table, traces):
    return pl.pallas_call(
        motion_kernel,
        out_shape=jax.ShapeDtypeStruct((OWNERS * PMAX, 2 * V), jnp.float32),
        grid_spec=pltpu.PrefetchScalarGridSpec(
            num_scalar_prefetch=1,
            grid=(NPER // QSTEP,),
            in_specs=[
                pl.BlockSpec((QSTEP, BLOCK, 3 * BLOCK), lambda s, place: (s, 0, 0)),
                pl.BlockSpec((BLOCK, NT // BLOCK * 2 * V), lambda s, place: (0, 0)),
            ],
            out_specs=pl.BlockSpec((OWNERS * PMAX, 2 * V), lambda s, place: (0, 0)),
            scratch_shapes=[pltpu.VMEM((3 * BLOCK, NT // BLOCK * 2 * V), jnp.bfloat16)],
        ),
        compiler_params=pltpu.CompilerParams(vmem_limit_bytes=VMEM),
        name="motion",
    )(place, table, traces)


def local(
    sgt_tensor, moment, slip_rate, footprint, live_blocks, start_delay, frequency, period_owner
):
    rupture = lax.axis_index("sgt") * OWNERS + lax.axis_index("work")
    outgoing = project(footprint.reshape(-1), sgt_tensor, moment)
    incoming = lax.all_to_all(outgoing, "sgt", split_axis=0, concat_axis=0, tiled=True)

    own_blocks = lax.dynamic_index_in_dim(footprint, rupture, 0, keepdims=False)
    own_count = lax.dynamic_index_in_dim(live_blocks, rupture, 0)
    own_delays = lax.dynamic_index_in_dim(start_delay, rupture, 0, keepdims=False)
    info = jnp.concatenate([own_count, own_blocks // HELD, own_delays])

    slips = jnp.transpose(slip_rate[0], (0, 2, 3, 1)).reshape(SLOTS, PB, L * V)
    zeros = jnp.zeros((SLOTS, PB, PHASES * V), slips.dtype)
    even = jnp.concatenate([zeros, slips, zeros], axis=2)
    odd = jnp.concatenate([zeros[..., V:], slips, zeros, zeros[..., :V]], axis=2)
    slips = jnp.stack([even, odd], axis=1)

    table = tables(frequency)
    period_ids = jnp.arange(NPER)
    same_owner = period_owner[:, None] == period_owner[None, :]
    earlier = period_ids[None, :] < period_ids[:, None]
    place = period_owner * PMAX + jnp.sum(same_owner & earlier, axis=1).astype(jnp.int32)

    traces = convolve(info, incoming.reshape(SLOTS, 2 * PB, NT), slips)
    peaks = motion(place, table, traces)
    peaks = lax.all_to_all(
        peaks.reshape(OWNERS, PMAX, 2 * V), "work", split_axis=0, concat_axis=0, tiled=True
    )
    result = jnp.transpose(peaks.reshape(OWNERS, PMAX, 2, V), (1, 2, 0, 3))
    return result[None]


def solution(mesh):
    in_specs = (
        P("sgt", None, None, None, None),
        P("sgt", None, None),
        P(("sgt", "work"), None, None, None, None),
        P(),
        P(),
        P(),
        P(),
        P(),
    )
    out_specs = P("work", None, None, "sgt", None)
    return jax.shard_map(local, mesh=mesh, in_specs=in_specs, out_specs=out_specs, check_vma=False)
```

```python
import functools
import math

import jax
import jax.numpy as jnp
from jax import lax
from jax.experimental import pallas as pl
from jax.experimental.pallas import tpu as pltpu
from jax.sharding import PartitionSpec as P

NT = 1024
L = 32
KIR = 512
V = 64
PB = 128
NPER = 44
SLOTS = 8
HELD = 4
NJ = 6
PMAX = 3
OWNERS = 16
damping = 0.05

PHASES = 4
TAPS = 9
PADROWS = 16
BLOCK = 256
SPAN = 128
TSTEP = 4
QSTEP = 11
SMALL = 12 * 1024 * 1024
LARGE = 28 * 1024 * 1024
PROJECT = 48 * 1024 * 1024

STEPS = ((0, 0), (0, 1), (2, 0), (2, 1), (1, 0), (3, 0), (1, 1), (3, 1))
GROUPS = ((0, 1), (2, 3), (4, 5), (6,), (7,))


def target(place, dz, dc):
    return ((place + 2 * dz) & 7) ^ dc


def origin(place, dz, dc):
    return ((place - 2 * dz) & 7) ^ dc


def project_block(weights, taken, scr, c):
    for i in range(0, PB, 16):
        total = None
        for j in range(NJ):
            term = weights[i : i + 16, j : j + 1] * taken[j, c, i : i + 16, :].astype(jnp.float32)
            total = term if total is None else total + term
        scr[c * PB + i : c * PB + i + 16, :] = total.astype(jnp.bfloat16)


def project_kernel(steps, fp_ref, sgt_ref, mom_ref, *rest):
    count = len(steps)
    outs, taken, scr, table, moments, in_sem, out_sem, small_sem = rest[:count], *rest[count:]
    fetch_table = pltpu.make_async_copy(fp_ref, table, small_sem.at[0])
    fetch_moments = pltpu.make_async_copy(mom_ref, moments, small_sem.at[1])
    fetch_table.start()
    fetch_moments.start()
    me = lax.axis_index("sgt")
    work = lax.axis_index("work")

    def load(n, c):
        return pltpu.make_async_copy(
            sgt_ref.at[n, :, c], taken.at[n, :, c], in_sem.at[2 * n + c]
        )

    for n in range(HELD):
        for c in range(2):
            load(n, c).start()
    fetch_table.wait()
    chosen = []
    for dz, dc in steps:
        rupture = target(me, dz, dc) * OWNERS + work
        found = jnp.int32(0)
        for k in range(SLOTS):
            block = table[k, rupture]
            found = jnp.where((block >> 2) == me, block & 3, found)
        chosen.append(found)
    fetch_moments.wait()

    @pl.loop(0, HELD)
    def _(n):
        weights = jnp.transpose(
            jnp.concatenate([moments[j, pl.ds(n, 1), :] for j in range(NJ)], axis=0)
        )
        for c in range(2):
            load(n, c).wait()
            project_block(weights, taken.at[n], scr.at[n], c)
        for m in range(count):
            copy = pltpu.make_async_copy(scr.at[n], outs[m], out_sem.at[m])
            pl.when(chosen[m] == n)(copy.start)

    for m in range(count):
        pltpu.make_async_copy(scr.at[0], outs[m], out_sem.at[m]).wait()


def project(steps, footprint, sgt_tensor, moment):
    count = len(steps)
    return pl.pallas_call(
        functools.partial(project_kernel, steps),
        out_shape=[jax.ShapeDtypeStruct((2 * PB, NT), jnp.bfloat16)] * count,
        in_specs=[
            pl.BlockSpec(memory_space=pl.ANY),
            pl.BlockSpec(memory_space=pl.ANY),
            pl.BlockSpec(memory_space=pl.ANY),
        ],
        out_specs=[pl.BlockSpec(memory_space=pltpu.VMEM)] * count,
        scratch_shapes=[
            pltpu.VMEM((HELD, NJ, 2, PB, NT), jnp.bfloat16),
            pltpu.VMEM((HELD, 2 * PB, NT), jnp.bfloat16),
            pltpu.SMEM((SLOTS, 128), jnp.int32),
            pltpu.VMEM((NJ, HELD, PB), jnp.float32),
            pltpu.SemaphoreType.DMA((2 * HELD,)),
            pltpu.SemaphoreType.DMA((count,)),
            pltpu.SemaphoreType.DMA((2,)),
        ],
        compiler_params=pltpu.CompilerParams(vmem_limit_bytes=PROJECT),
        cost_estimate=pl.CostEstimate(
            flops=HELD * 100000000, bytes_accessed=HELD * 3200000, transcendentals=0
        ),
        name="project",
    )(footprint.T, sgt_tensor, jnp.transpose(moment, (1, 0, 2)))


def tables_kernel(u_ref, v_ref, out_ref):
    step = pl.program_id(0)
    columns = jnp.transpose(u_ref[0])
    row = lax.broadcasted_iota(jnp.int32, (SPAN, SPAN), 0)
    lane = lax.broadcasted_iota(jnp.int32, (SPAN, SPAN), 1)
    source = ((lane & 31) << 2) + (lane >> 5)
    for n in range(TSTEP):
        sine = columns[:, 2 * n : 2 * n + 1]
        cosine = columns[:, 2 * n + 1 : 2 * n + 2]
        for j in range(3):
            span = slice(j * SPAN, (j + 1) * SPAN)
            value = sine * v_ref[0, 2 * n : 2 * n + 1, span] + (
                cosine * v_ref[0, 2 * n + 1 : 2 * n + 2, span]
            )
            if j == 0:
                value = jnp.where(row >= source, value, 0.0)
            if j == 2:
                value = jnp.where(row < source, value, 0.0)
            out_ref[n, :, span] = value.astype(jnp.bfloat16)
        state = 2 * (step * TSTEP + n)
        value = jnp.where(lane == state, sine, 0.0) + jnp.where(lane == state + 1, cosine, 0.0)
        out_ref[n, :, 3 * SPAN :] = value.astype(jnp.bfloat16)


def tables(frequency):
    angular = frequency[:, None]
    damped = angular * math.sqrt(1.0 - damping * damping)
    rows = jnp.arange(SPAN, dtype=jnp.float32)[None, :]
    decay = jnp.exp(-damping * angular * rows)
    u = jnp.stack([decay * jnp.sin(damped * rows), decay * jnp.cos(damped * rows)], axis=1)
    lane = jnp.arange(5 * SPAN)
    inner = lane % SPAN
    source = ((inner & 31) << 2) + (inner >> 5)
    before = jnp.asarray([0, 1, 4, 2, 3])[lane // SPAN]
    back = (source - before * SPAN).astype(jnp.float32)[None, :]
    growth = angular * angular / damped * jnp.exp(damping * angular * back)
    v = jnp.stack([growth * jnp.cos(damped * back), -growth * jnp.sin(damped * back)], axis=1)
    weights = v[..., 3 * SPAN :].reshape(2 * NPER, 2 * SPAN)
    weights = jnp.pad(weights, ((0, SPAN - 2 * NPER), (0, 0))).astype(jnp.bfloat16)
    steps = NPER // TSTEP
    table = pl.pallas_call(
        tables_kernel,
        out_shape=jax.ShapeDtypeStruct((NPER, SPAN, 4 * SPAN), jnp.bfloat16),
        grid=(steps,),
        in_specs=[
            pl.BlockSpec((1, 2 * TSTEP, SPAN), lambda s: (s, 0, 0)),
            pl.BlockSpec((1, 2 * TSTEP, 3 * SPAN), lambda s: (s, 0, 0)),
        ],
        out_specs=pl.BlockSpec((TSTEP, SPAN, 4 * SPAN), lambda s: (s, 0, 0)),
        compiler_params=pltpu.CompilerParams(vmem_limit_bytes=SMALL),
        cost_estimate=pl.CostEstimate(
            flops=NPER * 4 * SPAN * SPAN * 5, bytes_accessed=6000000, transcendentals=0
        ),
        name="tables",
    )(u.reshape(steps, 2 * TSTEP, SPAN), v[..., : 3 * SPAN].reshape(steps, 2 * TSTEP, 3 * SPAN))
    return table, weights


def gather_phases(delay, tensor_ref, phases):
    rows = lax.broadcasted_iota(jnp.int32, (BLOCK, 2 * BLOCK), 0)
    lane = lax.broadcasted_iota(jnp.int32, (BLOCK, 2 * BLOCK), 1)
    part = BLOCK // PHASES
    source = BLOCK + ((rows & 63) << 2) + (rows >> 6) - delay
    pick = jnp.where(lane == source, 1.0, 0.0).astype(jnp.bfloat16)
    for a in range(NT // BLOCK):
        low = max(a - 1, 0) * BLOCK
        window = tensor_ref[:, low : (a + 1) * BLOCK]
        chosen = pick[:, 2 * BLOCK - window.shape[1] :]
        moved = lax.dot_general(
            chosen, window, (((1,), (1,)), ((), ())), preferred_element_type=jnp.float32
        )
        for c in range(2):
            for b in range(PHASES):
                phases[
                    c, PADROWS + a * part : PADROWS + (a + 1) * part, b * PB : (b + 1) * PB
                ] = moved[b * part : (b + 1) * part, c * PB : (c + 1) * PB]


def histories(slips, slot, shift):
    pieces = []
    for b in range(PHASES):
        first = PHASES * shift - b
        low, high = max(first, 0), min(first + PHASES, L)
        if high <= low:
            pieces.append(jnp.zeros((PHASES * V, PB), jnp.bfloat16))
            continue
        parts = [slips[slot, low * V : high * V, :]]
        if low > first:
            parts.insert(0, jnp.zeros(((low - first) * V, PB), jnp.bfloat16))
        if high < first + PHASES:
            parts.append(jnp.zeros(((first + PHASES - high) * V, PB), jnp.bfloat16))
        pieces.append(parts[0] if len(parts) == 1 else jnp.concatenate(parts, axis=0))
    return jnp.concatenate(pieces, axis=1)


def convolve_kernel(arrivals, begins, info_ref, *rest):
    count = len(arrivals)
    tensors, slips, rest = rest[:count], rest[count], rest[count + 1 :]
    before = None
    if not begins:
        before, rest = rest[0], rest[1:]
    out_ref, phases = rest
    for half in range(2):
        phases[half, :, :PADROWS, :] = jnp.zeros((2, PADROWS, PHASES * PB), jnp.float32)
    for n in range(count):
        half = n % 2
        slot = info_ref[arrivals[n]]
        gather_phases(info_ref[SLOTS + arrivals[n]], tensors[n], phases.at[half])
        for c in range(2):
            rows = slice(c * BLOCK, (c + 1) * BLOCK)
            term = None
            for j in range(TAPS):
                shifted = phases[half, c, PADROWS - j : PADROWS - j + BLOCK, :]
                product = lax.dot_general(
                    shifted.astype(jnp.bfloat16),
                    histories(slips, slot, j),
                    (((1,), (1,)), ((), ())),
                    preferred_element_type=jnp.float32,
                )
                term = product if term is None else term + product
            if n > 0:
                out_ref[rows, :] += term
            elif begins:
                out_ref[rows, :] = term
            else:
                out_ref[rows, :] = before[rows, :] + term


def convolve(arrivals, info, tensors, slips, before):
    count = len(arrivals)
    vmem = pl.BlockSpec(memory_space=pltpu.VMEM)
    begins = before is None
    return pl.pallas_call(
        functools.partial(convolve_kernel, arrivals, begins),
        out_shape=jax.ShapeDtypeStruct((2 * BLOCK, PHASES * V), jnp.float32),
        in_specs=[pl.BlockSpec(memory_space=pltpu.SMEM)]
        + [vmem] * (count + 1)
        + ([] if begins else [vmem]),
        out_specs=vmem,
        scratch_shapes=[
            pltpu.VMEM((2, 2, PADROWS + BLOCK, PHASES * PB), jnp.float32),
        ],
        compiler_params=pltpu.CompilerParams(vmem_limit_bytes=LARGE),
        cost_estimate=pl.CostEstimate(
            flops=count * 1800000000, bytes_accessed=count * 1048576, transcendentals=0
        ),
        name="convolve",
    )(info, *tensors, slips, *([] if begins else [before]))


def motion_kernel(place_ref, table_ref, weights_ref, total, out_ref, traces, stacked):
    step = pl.program_id(0)
    spans = NT // SPAN
    wide = 2 * V
    width = spans * wide

    @pl.when(step == 0)
    def _():
        out_ref[...] = jnp.zeros_like(out_ref)
        part = SPAN // PHASES
        lane = lax.broadcasted_iota(jnp.int32, (part, wide), 1)
        for a in range(spans):
            for b in range(PHASES):
                half = slice((b // 2) * wide, (b // 2 + 1) * wide)
                first = total[a * part : (a + 1) * part, half]
                second = total[BLOCK + a * part : BLOCK + (a + 1) * part, half]
                if b % 2 == 0:
                    second = pltpu.roll(second, V, 1)
                else:
                    first = pltpu.roll(first, V, 1)
                traces[b * part : (b + 1) * part, a * wide : (a + 1) * wide] = jnp.where(
                    lane < V, first, second
                ).astype(jnp.bfloat16)
        stacked[:SPAN, :] = traces[...]
        for j, n in ((1, 1), (2, 4)):
            rows = slice(j * SPAN, (j + 1) * SPAN)
            stacked[rows, : n * wide] = jnp.zeros((SPAN, n * wide), jnp.bfloat16)
            stacked[rows, n * wide :] = traces[:, : width - n * wide]
        stacked[3 * SPAN :, : 2 * wide] = jnp.zeros((SPAN, 2 * wide), jnp.bfloat16)
        states = jnp.dot(
            weights_ref[...],
            stacked[: 2 * SPAN, : width - 2 * wide],
            preferred_element_type=jnp.float32,
        )
        stacked[3 * SPAN :, 2 * wide :] = states.astype(jnp.bfloat16)

    table = table_ref[...].reshape(QSTEP * SPAN, 4 * SPAN)
    early = jnp.dot(
        table[:, : 2 * SPAN],
        stacked[: 2 * SPAN, : 2 * wide],
        preferred_element_type=jnp.float32,
    )
    both = jnp.abs(early)
    for n in range(2, spans, 2):
        late = jnp.dot(
            table, stacked[:, n * wide : (n + 2) * wide], preferred_element_type=jnp.float32
        )
        both = jnp.maximum(both, jnp.abs(late))
    for n in range(QSTEP):
        highest = jnp.max(both[n * SPAN : (n + 1) * SPAN], axis=0, keepdims=True)
        highest = jnp.maximum(highest[:, :wide], highest[:, wide:])
        q = step * QSTEP + n
        out_ref[place_ref[q], pl.ds(place_ref[NPER + q], 1), :] = highest


def motion(place, table, weights, total):
    return pl.pallas_call(
        motion_kernel,
        out_shape=jax.ShapeDtypeStruct((OWNERS, PMAX, 2 * V), jnp.float32),
        grid_spec=pltpu.PrefetchScalarGridSpec(
            num_scalar_prefetch=1,
            grid=(NPER // QSTEP,),
            in_specs=[
                pl.BlockSpec((QSTEP, SPAN, 4 * SPAN), lambda s, place: (s, 0, 0)),
                pl.BlockSpec((SPAN, 2 * SPAN), lambda s, place: (0, 0)),
                pl.BlockSpec((2 * BLOCK, PHASES * V), lambda s, place: (0, 0)),
            ],
            out_specs=pl.BlockSpec((OWNERS, PMAX, 2 * V), lambda s, place: (0, 0, 0)),
            scratch_shapes=[
                pltpu.VMEM((SPAN, NT // SPAN * 2 * V), jnp.bfloat16),
                pltpu.VMEM((4 * SPAN, NT // SPAN * 2 * V), jnp.bfloat16),
            ],
        ),
        compiler_params=pltpu.CompilerParams(vmem_limit_bytes=SMALL),
        name="motion",
    )(place, table, weights, total)


def send(block, n):
    pairs = [(g, target(g, *STEPS[n])) for g in range(SLOTS)]
    return lax.ppermute(block, "sgt", pairs)


def local(
    sgt_tensor, moment, slip_rate, footprint, live_blocks, start_delay, frequency, period_owner
):
    here = lax.axis_index("sgt")
    rupture = here * OWNERS + lax.axis_index("work")
    outgoing = project(STEPS, footprint, sgt_tensor, moment)
    tensors = [outgoing[0]]
    for n in range(1, SLOTS - 1):
        tensors.append(send(outgoing[n], n))
    slip_rate, frequency, tensors[1] = lax.optimization_barrier(
        (slip_rate, frequency, tensors[1])
    )
    own_blocks = lax.dynamic_index_in_dim(footprint, rupture, 0, keepdims=False)
    own_count = lax.dynamic_index_in_dim(live_blocks, rupture, 0, keepdims=False)
    own_delays = lax.dynamic_index_in_dim(start_delay, rupture, 0, keepdims=False)
    origins = jnp.stack([origin(here, dz, dc) for dz, dc in STEPS])
    match = (own_blocks >> 2)[None, :] == origins[:, None]
    slot = jnp.sum(jnp.where(match, jnp.arange(SLOTS)[None, :], 0), axis=1)
    delay = jnp.sum(jnp.where(match, own_delays[None, :], 0), axis=1)
    info = jnp.concatenate([slot, jnp.where(slot < own_count, delay, 4 * NT)])

    slips = jnp.transpose(slip_rate[0], (0, 3, 1, 2)).reshape(SLOTS, L * V, PB)
    table, weights = tables(frequency)
    period_ids = jnp.arange(NPER)
    same_owner = period_owner[:, None] == period_owner[None, :]
    earlier = period_ids[None, :] < period_ids[:, None]
    rank = jnp.sum(same_owner & earlier, axis=1).astype(jnp.int32)
    place = jnp.concatenate([period_owner, rank])

    running = None
    for n, arrivals in enumerate(GROUPS):
        running = convolve(arrivals, info, [tensors[n] for n in arrivals], slips, running)
        if n == 0:
            last, running = lax.optimization_barrier((outgoing[SLOTS - 1], running))
            tensors.append(send(last, SLOTS - 1))
    peaks = motion(place, table, weights, running)
    peaks = lax.all_to_all(peaks, "work", split_axis=0, concat_axis=0, tiled=True)
    result = jnp.transpose(peaks.reshape(OWNERS, PMAX, 2, V), (1, 2, 0, 3))
    return result[None]


def solution(mesh):
    in_specs = (
        P("sgt", None, None, None, None),
        P("sgt", None, None),
        P(("sgt", "work"), None, None, None, None),
        P(),
        P(),
        P(),
        P(),
        P(),
    )
    out_specs = P("work", None, None, "sgt", None)
    return jax.shard_map(local, mesh=mesh, in_specs=in_specs, out_specs=out_specs, check_vma=False)
```

```python
import functools
import math

import jax
import jax.numpy as jnp
from jax import lax
from jax.experimental import pallas as pl
from jax.experimental.pallas import tpu as pltpu
from jax.sharding import PartitionSpec as P

NT = 1024
L = 32
KIR = 512
V = 64
PB = 128
NPER = 44
SLOTS = 8
HELD = 4
NJ = 6
PMAX = 3
OWNERS = 16
damping = 0.05

PHASES = 4
TAPS = 9
PADROWS = 16
BLOCK = 256
HALF = NT // 2
SPAN = 128
TSTEP = 4
QSTEP = 11
SMALL = 12 * 1024 * 1024
LARGE = 28 * 1024 * 1024
PROJECT = 60 * 1024 * 1024

STEPS = ((0, 0), (0, 1), (2, 0), (2, 1), (1, 0), (3, 0), (1, 1), (3, 1))
GROUPS = ((0, 1), (2, 3), (4, 5))


def target(place, dz, dc):
    return ((place + 2 * dz) & 7) ^ dc


def origin(place, dz, dc):
    return ((place - 2 * dz) & 7) ^ dc


def project_block(weights, taken, scr, c):
    for i in range(0, PB, 16):
        total = None
        for j in range(NJ):
            term = weights[i : i + 16, j : j + 1] * taken[j, c, i : i + 16, :].astype(jnp.float32)
            total = term if total is None else total + term
        scr[c * PB + i : c * PB + i + 16, :] = total.astype(jnp.bfloat16)


def pieces(steps):
    parts = []
    for n in range(len(steps)):
        if n < len(steps) - 2:
            parts.append((n, slice(0, NT)))
        else:
            parts += [(n, slice(0, HALF)), (n, slice(HALF, NT))]
    return parts


def project_kernel(steps, fp_ref, sgt_ref, mom_ref, *rest):
    parts = pieces(steps)
    outs, rest = rest[: len(parts)], rest[len(parts) :]
    taken, scr, table, moments, in_sem, out_sem, small_sem = rest
    fetch_table = pltpu.make_async_copy(fp_ref, table, small_sem.at[0])
    fetch_moments = pltpu.make_async_copy(mom_ref, moments, small_sem.at[1])
    fetch_table.start()
    fetch_moments.start()
    me = lax.axis_index("sgt")
    work = lax.axis_index("work")

    def load(n, c):
        return pltpu.make_async_copy(
            sgt_ref.at[n, :, c], taken.at[n, :, c], in_sem.at[2 * n + c]
        )

    for n in range(HELD):
        for c in range(2):
            load(n, c).start()
    fetch_table.wait()
    chosen = []
    for dz, dc in steps:
        rupture = target(me, dz, dc) * OWNERS + work
        found = jnp.int32(0)
        for k in range(SLOTS):
            block = table[k, rupture]
            found = jnp.where((block >> 2) == me, block & 3, found)
        chosen.append(found)
    fetch_moments.wait()

    @pl.loop(0, HELD)
    def _(n):
        weights = jnp.transpose(
            jnp.concatenate([moments[j, pl.ds(n, 1), :] for j in range(NJ)], axis=0)
        )
        for c in range(2):
            load(n, c).wait()
            project_block(weights, taken.at[n], scr.at[n], c)
        for m, (step, span) in enumerate(parts):
            copy = pltpu.make_async_copy(scr.at[n, :, span], outs[m], out_sem.at[m])
            pl.when(chosen[step] == n)(copy.start)

    for m, (step, span) in enumerate(parts):
        pltpu.make_async_copy(scr.at[0, :, span], outs[m], out_sem.at[m]).wait()


def project(steps, footprint, sgt_tensor, moment):
    parts = pieces(steps)
    return pl.pallas_call(
        functools.partial(project_kernel, steps),
        out_shape=[
            jax.ShapeDtypeStruct((2 * PB, span.stop - span.start), jnp.bfloat16) for _, span in parts
        ],
        in_specs=[
            pl.BlockSpec(memory_space=pl.ANY),
            pl.BlockSpec(memory_space=pl.ANY),
            pl.BlockSpec(memory_space=pl.ANY),
        ],
        out_specs=[pl.BlockSpec(memory_space=pl.ANY)] * len(parts),
        scratch_shapes=[
            pltpu.VMEM((HELD, NJ, 2, PB, NT), jnp.bfloat16),
            pltpu.VMEM((HELD, 2 * PB, NT), jnp.bfloat16),
            pltpu.SMEM((SLOTS, 128), jnp.int32),
            pltpu.VMEM((NJ, HELD, PB), jnp.float32),
            pltpu.SemaphoreType.DMA((2 * HELD,)),
            pltpu.SemaphoreType.DMA((len(parts),)),
            pltpu.SemaphoreType.DMA((2,)),
        ],
        compiler_params=pltpu.CompilerParams(vmem_limit_bytes=PROJECT),
        cost_estimate=pl.CostEstimate(
            flops=HELD * 100000000, bytes_accessed=HELD * 3200000, transcendentals=0
        ),
        name="project",
    )(footprint.T, sgt_tensor, jnp.transpose(moment, (1, 0, 2)))


def tables_kernel(u_ref, v_ref, out_ref):
    step = pl.program_id(0)
    columns = jnp.transpose(u_ref[0])
    row = lax.broadcasted_iota(jnp.int32, (SPAN, SPAN), 0)
    lane = lax.broadcasted_iota(jnp.int32, (SPAN, SPAN), 1)
    source = ((lane & 31) << 2) + (lane >> 5)
    for n in range(TSTEP):
        sine = columns[:, 2 * n : 2 * n + 1]
        cosine = columns[:, 2 * n + 1 : 2 * n + 2]
        for j in range(3):
            span = slice(j * SPAN, (j + 1) * SPAN)
            value = sine * v_ref[0, 2 * n : 2 * n + 1, span] + (
                cosine * v_ref[0, 2 * n + 1 : 2 * n + 2, span]
            )
            if j == 0:
                value = jnp.where(row >= source, value, 0.0)
            if j == 2:
                value = jnp.where(row < source, value, 0.0)
            out_ref[n, :, span] = value.astype(jnp.bfloat16)
        state = 2 * (step * TSTEP + n)
        value = jnp.where(lane == state, sine, 0.0) + jnp.where(lane == state + 1, cosine, 0.0)
        out_ref[n, :, 3 * SPAN :] = value.astype(jnp.bfloat16)


def tables(frequency):
    angular = frequency[:, None]
    damped = angular * math.sqrt(1.0 - damping * damping)
    rows = jnp.arange(SPAN, dtype=jnp.float32)[None, :]
    decay = jnp.exp(-damping * angular * rows)
    u = jnp.stack([decay * jnp.sin(damped * rows), decay * jnp.cos(damped * rows)], axis=1)
    lane = jnp.arange(5 * SPAN)
    inner = lane % SPAN
    source = ((inner & 31) << 2) + (inner >> 5)
    before = jnp.asarray([0, 1, 4, 2, 3])[lane // SPAN]
    back = (source - before * SPAN).astype(jnp.float32)[None, :]
    growth = angular * angular / damped * jnp.exp(damping * angular * back)
    v = jnp.stack([growth * jnp.cos(damped * back), -growth * jnp.sin(damped * back)], axis=1)
    weights = v[..., 3 * SPAN :].reshape(2 * NPER, 2 * SPAN)
    weights = jnp.pad(weights, ((0, SPAN - 2 * NPER), (0, 0))).astype(jnp.bfloat16)
    steps = NPER // TSTEP
    table = pl.pallas_call(
        tables_kernel,
        out_shape=jax.ShapeDtypeStruct((NPER, SPAN, 4 * SPAN), jnp.bfloat16),
        grid=(steps,),
        in_specs=[
            pl.BlockSpec((1, 2 * TSTEP, SPAN), lambda s: (s, 0, 0)),
            pl.BlockSpec((1, 2 * TSTEP, 3 * SPAN), lambda s: (s, 0, 0)),
        ],
        out_specs=pl.BlockSpec((TSTEP, SPAN, 4 * SPAN), lambda s: (s, 0, 0)),
        compiler_params=pltpu.CompilerParams(vmem_limit_bytes=SMALL),
        cost_estimate=pl.CostEstimate(
            flops=NPER * 4 * SPAN * SPAN * 5, bytes_accessed=6000000, transcendentals=0
        ),
        name="tables",
    )(u.reshape(steps, 2 * TSTEP, SPAN), v[..., : 3 * SPAN].reshape(steps, 2 * TSTEP, 3 * SPAN))
    return table, weights


def gather_phases(delay, tensor_ref, phases):
    rows = lax.broadcasted_iota(jnp.int32, (BLOCK, 2 * BLOCK), 0)
    lane = lax.broadcasted_iota(jnp.int32, (BLOCK, 2 * BLOCK), 1)
    part = BLOCK // PHASES
    source = BLOCK + ((rows & 63) << 2) + (rows >> 6) - delay
    pick = jnp.where(lane == source, 1.0, 0.0).astype(jnp.bfloat16)
    for a in range(NT // BLOCK):
        low = max(a - 1, 0) * BLOCK
        window = tensor_ref[:, low : (a + 1) * BLOCK]
        chosen = pick[:, 2 * BLOCK - window.shape[1] :]
        moved = lax.dot_general(
            chosen, window, (((1,), (1,)), ((), ())), preferred_element_type=jnp.float32
        )
        for c in range(2):
            for b in range(PHASES):
                phases[
                    c, PADROWS + a * part : PADROWS + (a + 1) * part, b * PB : (b + 1) * PB
                ] = moved[b * part : (b + 1) * part, c * PB : (c + 1) * PB]


def histories(slips, slot, shift):
    pieces = []
    for b in range(PHASES):
        first = PHASES * shift - b
        low, high = max(first, 0), min(first + PHASES, L)
        if high <= low:
            pieces.append(jnp.zeros((PHASES * V, PB), jnp.bfloat16))
            continue
        parts = [slips[slot, low * V : high * V, :]]
        if low > first:
            parts.insert(0, jnp.zeros(((low - first) * V, PB), jnp.bfloat16))
        if high < first + PHASES:
            parts.append(jnp.zeros(((first + PHASES - high) * V, PB), jnp.bfloat16))
        pieces.append(parts[0] if len(parts) == 1 else jnp.concatenate(parts, axis=0))
    return jnp.concatenate(pieces, axis=1)


def convolve_kernel(arrivals, begins, info_ref, *rest):
    count = len(arrivals)
    tensors, slips, rest = rest[:count], rest[count], rest[count + 1 :]
    before = None
    if not begins:
        before, rest = rest[0], rest[1:]
    out_ref, phases = rest
    for half in range(2):
        phases[half, :, :PADROWS, :] = jnp.zeros((2, PADROWS, PHASES * PB), jnp.float32)
    for n in range(count):
        half = n % 2
        slot = info_ref[arrivals[n]]
        gather_phases(info_ref[SLOTS + arrivals[n]], tensors[n], phases.at[half])
        for c in range(2):
            rows = slice(c * BLOCK, (c + 1) * BLOCK)
            term = None
            for j in range(TAPS):
                shifted = phases[half, c, PADROWS - j : PADROWS - j + BLOCK, :]
                product = lax.dot_general(
                    shifted.astype(jnp.bfloat16),
                    histories(slips, slot, j),
                    (((1,), (1,)), ((), ())),
                    preferred_element_type=jnp.float32,
                )
                term = product if term is None else term + product
            if n > 0:
                out_ref[rows, :] += term
            elif begins:
                out_ref[rows, :] = term
            else:
                out_ref[rows, :] = before[rows, :] + term


def convolve(arrivals, info, tensors, slips, before):
    count = len(arrivals)
    vmem = pl.BlockSpec(memory_space=pltpu.VMEM)
    begins = before is None
    return pl.pallas_call(
        functools.partial(convolve_kernel, arrivals, begins),
        out_shape=jax.ShapeDtypeStruct((2 * BLOCK, PHASES * V), jnp.float32),
        in_specs=[pl.BlockSpec(memory_space=pltpu.SMEM)]
        + [vmem] * (count + 1)
        + ([] if begins else [vmem]),
        out_specs=vmem,
        scratch_shapes=[
            pltpu.VMEM((2, 2, PADROWS + BLOCK, PHASES * PB), jnp.float32),
        ],
        compiler_params=pltpu.CompilerParams(vmem_limit_bytes=LARGE),
        cost_estimate=pl.CostEstimate(
            flops=count * 1800000000, bytes_accessed=count * 1048576, transcendentals=0
        ),
        name="convolve",
    )(info, *tensors, slips, *([] if begins else [before]))


def pick_phases(delay):
    rows = lax.broadcasted_iota(jnp.int32, (BLOCK, 2 * BLOCK), 0)
    lane = lax.broadcasted_iota(jnp.int32, (BLOCK, 2 * BLOCK), 1)
    source = BLOCK + ((rows & 63) << 2) + (rows >> 6) - delay
    return jnp.where(lane == source, 1.0, 0.0).astype(jnp.bfloat16)


def gather_some(delay, blocks, chunks, phases):
    pick = pick_phases(delay)
    part = BLOCK // PHASES
    dims = (((1,), (1,)), ((), ()))
    for place, a in enumerate(chunks):
        moved = lax.dot_general(
            pick[:, BLOCK:], blocks[a], dims, preferred_element_type=jnp.float32
        )
        if a > 0:
            moved += lax.dot_general(
                pick[:, :BLOCK], blocks[a - 1], dims, preferred_element_type=jnp.float32
            )
        low = PADROWS + place * part
        for c in range(2):
            for b in range(PHASES):
                phases[c, low : low + part, b * PB : (b + 1) * PB] = moved[
                    b * part : (b + 1) * part, c * PB : (c + 1) * PB
                ]


def finish_kernel(late, info_ref, place_ref, *rest):
    count = 4 if late else 2
    tensors, rest = rest[:count], rest[count:]
    slips, before, table_ref, weights_ref = rest[:4]
    rest = rest[4:]
    known, peaks = None, None
    if late:
        known, peaks = rest[:2]
        rest = rest[2:]
    out_ref, traces = rest[0], rest[1]
    phases, total, stacked = rest[2:]
    rows = BLOCK // 2
    wide = 2 * V
    first_row = PADROWS + (64 if late else 0)
    if not late:
        phases[:, :, :PADROWS, :] = jnp.zeros((2, 2, PADROWS, PHASES * PB), jnp.float32)
    for n in range(2):
        arrival = SLOTS - 2 + n
        slot = info_ref[arrival]
        halves = tensors[2 * n : 2 * n + 2] if late else tensors[n : n + 1]
        blocks = [half[:, i * BLOCK : (i + 1) * BLOCK] for half in halves for i in range(2)]
        chunks = (1, 2, 3) if late else (0, 1)
        gather_some(info_ref[SLOTS + arrival], blocks, chunks, phases.at[n])
        term = None
        for j in range(TAPS):
            shifted = jnp.concatenate(
                [phases[n, c, first_row - j : first_row - j + rows, :] for c in range(2)], axis=0
            )
            product = lax.dot_general(
                shifted.astype(jnp.bfloat16),
                histories(slips, slot, j),
                (((1,), (1,)), ((), ())),
                preferred_element_type=jnp.float32,
            )
            term = product if term is None else term + product
        if n == 0:
            for c in range(2):
                low = c * BLOCK + (rows if late else 0)
                total[c * rows : (c + 1) * rows, :] = (
                    before[low : low + rows, :] + term[c * rows : (c + 1) * rows, :]
                )
        else:
            total[...] += term

    part = SPAN // PHASES
    spans = rows // part
    lane = lax.broadcasted_iota(jnp.int32, (part, wide), 1)
    for a in range(spans):
        for b in range(PHASES):
            half = slice((b // 2) * wide, (b // 2 + 1) * wide)
            first = total[a * part : (a + 1) * part, half]
            second = total[rows + a * part : rows + (a + 1) * part, half]
            if b % 2 == 0:
                second = pltpu.roll(second, V, 1)
            else:
                first = pltpu.roll(first, V, 1)
            traces[b * part : (b + 1) * part, a * wide : (a + 1) * wide] = jnp.where(
                lane < V, first, second
            ).astype(jnp.bfloat16)

    width = spans * wide
    nothing = jnp.zeros((SPAN, width), jnp.bfloat16)
    stacked[:SPAN, :] = traces[...]
    stacked[SPAN : 2 * SPAN, wide:] = traces[:, : width - wide]
    if late:
        stacked[SPAN : 2 * SPAN, :wide] = known[:, width - wide :]
        stacked[2 * SPAN : 3 * SPAN, :] = known[...]
        near = jnp.concatenate([known[:, 2 * wide :], traces[:, : 2 * wide]], axis=1)
        far = jnp.concatenate([known[:, wide:], traces[:, :wide]], axis=1)
        low = 0
    else:
        stacked[SPAN : 2 * SPAN, :wide] = nothing[:, :wide]
        stacked[2 * SPAN : 3 * SPAN, :] = nothing
        stacked[3 * SPAN :, : 2 * wide] = nothing[:, : 2 * wide]
        near = traces[:, : 2 * wide]
        far = jnp.concatenate([nothing[:, :wide], traces[:, :wide]], axis=1)
        low = 2 * wide
    states = jnp.dot(
        weights_ref[...],
        jnp.concatenate([near, far], axis=0),
        preferred_element_type=jnp.float32,
    )
    stacked[3 * SPAN :, low:] = states.astype(jnp.bfloat16)
    out_ref[...] = peaks[...] if late else jnp.zeros_like(out_ref)

    @pl.loop(0, NPER // QSTEP)
    def _(step):
        table = table_ref[pl.ds(step * QSTEP, QSTEP)].reshape(QSTEP * SPAN, 4 * SPAN)
        deep = 4 * SPAN if late else 2 * SPAN
        one = jnp.dot(
            table[:, :deep], stacked[:deep, : 2 * wide], preferred_element_type=jnp.float32
        )
        two = jnp.dot(table, stacked[:, 2 * wide :], preferred_element_type=jnp.float32)
        both = jnp.maximum(jnp.abs(one), jnp.abs(two))
        for n in range(QSTEP):
            highest = jnp.max(both[n * SPAN : (n + 1) * SPAN], axis=0, keepdims=True)
            highest = jnp.maximum(highest[:, :wide], highest[:, wide:])
            q = step * QSTEP + n
            owner, rank = place_ref[q], place_ref[NPER + q]
            if late:
                highest = jnp.maximum(highest, peaks[owner, pl.ds(rank, 1), :])
            out_ref[owner, pl.ds(rank, 1), :] = highest


def finish(late, info, place, tensors, slips, before, table, weights, known):
    smem = pl.BlockSpec(memory_space=pltpu.SMEM)
    vmem = pl.BlockSpec(memory_space=pltpu.VMEM)
    operands = [*tensors, slips, before, table, weights, *known]
    out_shape = [jax.ShapeDtypeStruct((OWNERS, PMAX, 2 * V), jnp.float32)]
    traces = (SPAN, HALF // SPAN * 2 * V)
    scratch = []
    if late:
        scratch = [pltpu.VMEM(traces, jnp.bfloat16)]
    else:
        out_shape.append(jax.ShapeDtypeStruct(traces, jnp.bfloat16))
    held = PADROWS + (192 if late else 128)
    return pl.pallas_call(
        functools.partial(finish_kernel, late),
        out_shape=out_shape,
        in_specs=[smem, smem] + [vmem] * len(operands),
        out_specs=[vmem] * len(out_shape),
        scratch_shapes=scratch
        + [
            pltpu.VMEM((2, 2, held, PHASES * PB), jnp.float32),
            pltpu.VMEM((BLOCK, PHASES * V), jnp.float32),
            pltpu.VMEM((4 * SPAN, HALF // SPAN * 2 * V), jnp.bfloat16),
        ],
        compiler_params=pltpu.CompilerParams(vmem_limit_bytes=LARGE),
        cost_estimate=pl.CostEstimate(
            flops=3600000000, bytes_accessed=8000000, transcendentals=0
        ),
        name="finish",
    )(info, place, *operands)


def send(block, n):
    pairs = [(g, target(g, *STEPS[n])) for g in range(SLOTS)]
    return lax.ppermute(block, "sgt", pairs)


def local(
    sgt_tensor, moment, slip_rate, footprint, live_blocks, start_delay, frequency, period_owner
):
    here = lax.axis_index("sgt")
    rupture = here * OWNERS + lax.axis_index("work")
    outgoing = list(project(STEPS, footprint, sgt_tensor, moment))
    tensors = [outgoing[0]]
    for n in range(1, SLOTS - 2):
        tensors.append(send(outgoing[n], n))
    first, second = SLOTS - 2, SLOTS - 1
    halves = {first: [], second: []}

    def send_after(part, n, arrived):
        block, tensors[arrived] = lax.optimization_barrier((outgoing[part], tensors[arrived]))
        halves[n].append(send(block, n))

    send_after(SLOTS - 2, first, 1)
    send_after(SLOTS, second, 2)
    slip_rate, frequency, tensors[1] = lax.optimization_barrier(
        (slip_rate, frequency, tensors[1])
    )
    own_blocks = lax.dynamic_index_in_dim(footprint, rupture, 0, keepdims=False)
    own_count = lax.dynamic_index_in_dim(live_blocks, rupture, 0, keepdims=False)
    own_delays = lax.dynamic_index_in_dim(start_delay, rupture, 0, keepdims=False)
    origins = jnp.stack([origin(here, dz, dc) for dz, dc in STEPS])
    match = (own_blocks >> 2)[None, :] == origins[:, None]
    slot = jnp.sum(jnp.where(match, jnp.arange(SLOTS)[None, :], 0), axis=1)
    delay = jnp.sum(jnp.where(match, own_delays[None, :], 0), axis=1)
    info = jnp.concatenate([slot, jnp.where(slot < own_count, delay, 4 * NT)])

    slips = jnp.transpose(slip_rate[0], (0, 3, 1, 2)).reshape(SLOTS, L * V, PB)
    table, weights = tables(frequency)
    period_ids = jnp.arange(NPER)
    same_owner = period_owner[:, None] == period_owner[None, :]
    earlier = period_ids[None, :] < period_ids[:, None]
    rank = jnp.sum(same_owner & earlier, axis=1).astype(jnp.int32)
    place = jnp.concatenate([period_owner, rank])

    running = None
    for n, arrivals in enumerate(GROUPS):
        running = convolve(arrivals, info, [tensors[n] for n in arrivals], slips, running)
        if n == 1:
            outgoing[SLOTS - 1], outgoing[SLOTS + 1], running, table = lax.optimization_barrier(
                (outgoing[SLOTS - 1], outgoing[SLOTS + 1], running, table)
            )
            send_after(SLOTS - 1, first, 4)
            send_after(SLOTS + 1, second, 5)
    peaks, known = finish(
        False,
        info,
        place,
        [halves[first][0], halves[second][0]],
        slips,
        running,
        table,
        weights,
        [],
    )
    (peaks,) = finish(
        True,
        info,
        place,
        halves[first] + halves[second],
        slips,
        running,
        table,
        weights,
        [known, peaks],
    )
    peaks = lax.all_to_all(peaks, "work", split_axis=0, concat_axis=0, tiled=True)
    result = jnp.transpose(peaks.reshape(OWNERS, PMAX, 2, V), (1, 2, 0, 3))
    return result[None]


def solution(mesh):
    in_specs = (
        P("sgt", None, None, None, None),
        P("sgt", None, None),
        P(("sgt", "work"), None, None, None, None),
        P(),
        P(),
        P(),
        P(),
        P(),
    )
    out_specs = P("work", None, None, "sgt", None)
    return jax.shard_map(local, mesh=mesh, in_specs=in_specs, out_specs=out_specs, check_vma=False)
```

```python
import functools
import math

import jax
import jax.numpy as jnp
from jax import lax
from jax.experimental import pallas as pl
from jax.experimental.pallas import tpu as pltpu
from jax.sharding import PartitionSpec as P

NT = 1024
L = 32
KIR = 512
V = 64
PB = 128
NPER = 44
SLOTS = 8
HELD = 4
NJ = 6
PMAX = 3
OWNERS = 16
damping = 0.05

PHASES = 4
TAPS = 9
PADROWS = 16
BLOCK = 256
HALF = NT // 2
SPAN = 128
TSTEP = 4
QSTEP = 22
SMALL = 12 * 1024 * 1024
LARGE = 28 * 1024 * 1024
PROJECT = 60 * 1024 * 1024

STEPS = ((0, 0), (0, 1), (2, 0), (2, 1), (1, 0), (3, 0), (1, 1), (3, 1))
GROUPS = ((0, 1), (2, 3), (4, 5))


def target(place, dz, dc):
    return ((place + 2 * dz) & 7) ^ dc


def origin(place, dz, dc):
    return ((place - 2 * dz) & 7) ^ dc


def project_block(weights, taken, scr, c):
    for i in range(0, PB, 16):
        total = None
        for j in range(NJ):
            term = weights[i : i + 16, j : j + 1] * taken[j, c, i : i + 16, :].astype(jnp.float32)
            total = term if total is None else total + term
        scr[c * PB + i : c * PB + i + 16, :] = total.astype(jnp.bfloat16)


def pieces(steps):
    parts = []
    for n in range(len(steps)):
        if n < len(steps) - 2:
            parts.append((n, slice(0, NT)))
        else:
            parts += [(n, slice(0, HALF)), (n, slice(HALF, NT))]
    return parts


def project_kernel(steps, fp_ref, sgt_ref, mom_ref, *rest):
    parts = pieces(steps)
    outs, rest = rest[: len(parts)], rest[len(parts) :]
    taken, scr, table, chosen, moments, in_sem, out_sem, small_sem = rest
    fetch_table = pltpu.make_async_copy(fp_ref, table, small_sem.at[0])
    fetch_moments = pltpu.make_async_copy(mom_ref, moments, small_sem.at[1])
    fetch_moments.start()
    fetch_table.start()
    me = lax.axis_index("sgt")
    work = lax.axis_index("work")

    def load(n, c):
        return pltpu.make_async_copy(
            sgt_ref.at[n, :, c], taken.at[n, :, c], in_sem.at[2 * n + c]
        )

    for n in range(HELD):
        for c in range(2):
            load(n, c).start()
    fetch_moments.wait()

    @pl.loop(0, HELD)
    def _(n):
        weights = jnp.transpose(
            jnp.concatenate([moments[j, pl.ds(n, 1), :] for j in range(NJ)], axis=0)
        )
        for c in range(2):
            load(n, c).wait()
            project_block(weights, taken.at[n], scr.at[n], c)

        @pl.when(n == 0)
        def _():
            fetch_table.wait()
            for m, (dz, dc) in enumerate(steps):
                rupture = target(me, dz, dc) * OWNERS + work
                found = jnp.int32(0)
                for k in range(SLOTS):
                    block = table[k, rupture]
                    found = jnp.where((block >> 2) == me, block & 3, found)
                chosen[m] = found

        for m, (step, span) in enumerate(parts):
            copy = pltpu.make_async_copy(scr.at[n, :, span], outs[m], out_sem.at[m])
            pl.when(chosen[step] == n)(copy.start)

    for m, (step, span) in enumerate(parts):
        pltpu.make_async_copy(scr.at[0, :, span], outs[m], out_sem.at[m]).wait()


def project(steps, footprint, sgt_tensor, moment):
    parts = pieces(steps)
    return pl.pallas_call(
        functools.partial(project_kernel, steps),
        out_shape=[
            jax.ShapeDtypeStruct((2 * PB, span.stop - span.start), jnp.bfloat16) for _, span in parts
        ],
        in_specs=[
            pl.BlockSpec(memory_space=pl.ANY),
            pl.BlockSpec(memory_space=pl.ANY),
            pl.BlockSpec(memory_space=pl.ANY),
        ],
        out_specs=[pl.BlockSpec(memory_space=pl.ANY)] * len(parts),
        scratch_shapes=[
            pltpu.VMEM((HELD, NJ, 2, PB, NT), jnp.bfloat16),
            pltpu.VMEM((HELD, 2 * PB, NT), jnp.bfloat16),
            pltpu.SMEM((SLOTS, 128), jnp.int32),
            pltpu.SMEM((SLOTS,), jnp.int32),
            pltpu.VMEM((NJ, HELD, PB), jnp.float32),
            pltpu.SemaphoreType.DMA((2 * HELD,)),
            pltpu.SemaphoreType.DMA((len(parts),)),
            pltpu.SemaphoreType.DMA((2,)),
        ],
        compiler_params=pltpu.CompilerParams(vmem_limit_bytes=PROJECT),
        cost_estimate=pl.CostEstimate(
            flops=HELD * 100000000, bytes_accessed=HELD * 3200000, transcendentals=0
        ),
        name="project",
    )(footprint.T, sgt_tensor, jnp.transpose(moment, (1, 0, 2)))


def tables_kernel(u_ref, v_ref, out_ref):
    step = pl.program_id(0)
    columns = jnp.transpose(u_ref[0])
    row = lax.broadcasted_iota(jnp.int32, (SPAN, SPAN), 0)
    lane = lax.broadcasted_iota(jnp.int32, (SPAN, SPAN), 1)
    source = ((lane & 31) << 2) + (lane >> 5)
    for n in range(TSTEP):
        sine = columns[:, 2 * n : 2 * n + 1]
        cosine = columns[:, 2 * n + 1 : 2 * n + 2]
        for j in range(3):
            span = slice(j * SPAN, (j + 1) * SPAN)
            value = sine * v_ref[0, 2 * n : 2 * n + 1, span] + (
                cosine * v_ref[0, 2 * n + 1 : 2 * n + 2, span]
            )
            if j == 0:
                value = jnp.where(row >= source, value, 0.0)
            if j == 2:
                value = jnp.where(row < source, value, 0.0)
            out_ref[n, :, span] = value.astype(jnp.bfloat16)
        state = 2 * (step * TSTEP + n)
        value = jnp.where(lane == state, sine, 0.0) + jnp.where(lane == state + 1, cosine, 0.0)
        out_ref[n, :, 3 * SPAN :] = value.astype(jnp.bfloat16)


def tables(frequency):
    angular = frequency[:, None]
    damped = angular * math.sqrt(1.0 - damping * damping)
    rows = jnp.arange(SPAN, dtype=jnp.float32)[None, :]
    decay = jnp.exp(-damping * angular * rows)
    u = jnp.stack([decay * jnp.sin(damped * rows), decay * jnp.cos(damped * rows)], axis=1)
    lane = jnp.arange(5 * SPAN)
    inner = lane % SPAN
    source = ((inner & 31) << 2) + (inner >> 5)
    before = jnp.asarray([0, 1, 4, 2, 3])[lane // SPAN]
    back = (source - before * SPAN).astype(jnp.float32)[None, :]
    growth = angular * angular / damped * jnp.exp(damping * angular * back)
    v = jnp.stack([growth * jnp.cos(damped * back), -growth * jnp.sin(damped * back)], axis=1)
    weights = v[..., 3 * SPAN :].reshape(2 * NPER, 2 * SPAN)
    weights = jnp.pad(weights, ((0, SPAN - 2 * NPER), (0, 0))).astype(jnp.bfloat16)
    steps = NPER // TSTEP
    table = pl.pallas_call(
        tables_kernel,
        out_shape=jax.ShapeDtypeStruct((NPER, SPAN, 4 * SPAN), jnp.bfloat16),
        grid=(steps,),
        in_specs=[
            pl.BlockSpec((1, 2 * TSTEP, SPAN), lambda s: (s, 0, 0)),
            pl.BlockSpec((1, 2 * TSTEP, 3 * SPAN), lambda s: (s, 0, 0)),
        ],
        out_specs=pl.BlockSpec((TSTEP, SPAN, 4 * SPAN), lambda s: (s, 0, 0)),
        compiler_params=pltpu.CompilerParams(vmem_limit_bytes=SMALL),
        cost_estimate=pl.CostEstimate(
            flops=NPER * 4 * SPAN * SPAN * 5, bytes_accessed=6000000, transcendentals=0
        ),
        name="tables",
    )(u.reshape(steps, 2 * TSTEP, SPAN), v[..., : 3 * SPAN].reshape(steps, 2 * TSTEP, 3 * SPAN))
    return table, weights


def gather_phases(delay, tensor_ref, phases):
    rows = lax.broadcasted_iota(jnp.int32, (BLOCK, 2 * BLOCK), 0)
    lane = lax.broadcasted_iota(jnp.int32, (BLOCK, 2 * BLOCK), 1)
    part = BLOCK // PHASES
    source = BLOCK + ((rows & 63) << 2) + (rows >> 6) - delay
    pick = jnp.where(lane == source, 1.0, 0.0).astype(jnp.bfloat16)
    for a in range(NT // BLOCK):
        low = max(a - 1, 0) * BLOCK
        window = tensor_ref[:, low : (a + 1) * BLOCK]
        chosen = pick[:, 2 * BLOCK - window.shape[1] :]
        moved = lax.dot_general(
            chosen, window, (((1,), (1,)), ((), ())), preferred_element_type=jnp.float32
        )
        for c in range(2):
            for b in range(PHASES):
                phases[
                    c, PADROWS + a * part : PADROWS + (a + 1) * part, b * PB : (b + 1) * PB
                ] = moved[b * part : (b + 1) * part, c * PB : (c + 1) * PB]


def histories(slips, slot, shift):
    pieces = []
    for b in range(PHASES):
        first = PHASES * shift - b
        low, high = max(first, 0), min(first + PHASES, L)
        if high <= low:
            pieces.append(jnp.zeros((PHASES * V, PB), jnp.bfloat16))
            continue
        parts = [slips[slot, low * V : high * V, :]]
        if low > first:
            parts.insert(0, jnp.zeros(((low - first) * V, PB), jnp.bfloat16))
        if high < first + PHASES:
            parts.append(jnp.zeros(((first + PHASES - high) * V, PB), jnp.bfloat16))
        pieces.append(parts[0] if len(parts) == 1 else jnp.concatenate(parts, axis=0))
    return jnp.concatenate(pieces, axis=1)


def convolve_kernel(arrivals, begins, info_ref, *rest):
    count = len(arrivals)
    tensors, slips, rest = rest[:count], rest[count], rest[count + 1 :]
    before = None
    if not begins:
        before, rest = rest[0], rest[1:]
    out_ref, phases = rest
    for half in range(2):
        phases[half, :, :PADROWS, :] = jnp.zeros((2, PADROWS, PHASES * PB), jnp.float32)
    for n in range(count):
        half = n % 2
        slot = info_ref[arrivals[n]]
        gather_phases(info_ref[SLOTS + arrivals[n]], tensors[n], phases.at[half])
        for c in range(2):
            rows = slice(c * BLOCK, (c + 1) * BLOCK)
            term = None
            for j in range(TAPS):
                shifted = phases[half, c, PADROWS - j : PADROWS - j + BLOCK, :]
                product = lax.dot_general(
                    shifted.astype(jnp.bfloat16),
                    histories(slips, slot, j),
                    (((1,), (1,)), ((), ())),
                    preferred_element_type=jnp.float32,
                )
                term = product if term is None else term + product
            if n > 0:
                out_ref[rows, :] += term
            elif begins:
                out_ref[rows, :] = term
            else:
                out_ref[rows, :] = before[rows, :] + term


def convolve(arrivals, info, tensors, slips, before):
    count = len(arrivals)
    vmem = pl.BlockSpec(memory_space=pltpu.VMEM)
    begins = before is None
    return pl.pallas_call(
        functools.partial(convolve_kernel, arrivals, begins),
        out_shape=jax.ShapeDtypeStruct((2 * BLOCK, PHASES * V), jnp.float32),
        in_specs=[pl.BlockSpec(memory_space=pltpu.SMEM)]
        + [vmem] * (count + 1)
        + ([] if begins else [vmem]),
        out_specs=vmem,
        scratch_shapes=[
            pltpu.VMEM((2, 2, PADROWS + BLOCK, PHASES * PB), jnp.float32),
        ],
        compiler_params=pltpu.CompilerParams(vmem_limit_bytes=LARGE),
        cost_estimate=pl.CostEstimate(
            flops=count * 1800000000, bytes_accessed=count * 1048576, transcendentals=0
        ),
        name="convolve",
    )(info, *tensors, slips, *([] if begins else [before]))


def pick_phases(delay):
    rows = lax.broadcasted_iota(jnp.int32, (BLOCK, 2 * BLOCK), 0)
    lane = lax.broadcasted_iota(jnp.int32, (BLOCK, 2 * BLOCK), 1)
    source = BLOCK + ((rows & 63) << 2) + (rows >> 6) - delay
    return jnp.where(lane == source, 1.0, 0.0).astype(jnp.bfloat16)


def gather_some(delay, blocks, chunks, phases):
    pick = pick_phases(delay)
    part = BLOCK // PHASES
    dims = (((1,), (1,)), ((), ()))
    for place, a in enumerate(chunks):
        moved = lax.dot_general(
            pick[:, BLOCK:], blocks[a], dims, preferred_element_type=jnp.float32
        )
        if a > 0:
            moved += lax.dot_general(
                pick[:, :BLOCK], blocks[a - 1], dims, preferred_element_type=jnp.float32
            )
        low = PADROWS + place * part
        for c in range(2):
            for b in range(PHASES):
                phases[c, low : low + part, b * PB : (b + 1) * PB] = moved[
                    b * part : (b + 1) * part, c * PB : (c + 1) * PB
                ]


def finish_kernel(late, info_ref, place_ref, *rest):
    count = 4 if late else 2
    tensors, rest = rest[:count], rest[count:]
    slips, before, table_ref, weights_ref = rest[:4]
    rest = rest[4:]
    known, peaks = None, None
    if late:
        known, peaks = rest[:2]
        rest = rest[2:]
    out_ref, traces = rest[0], rest[1]
    phases, total, stacked = rest[2:]
    rows = BLOCK // 2
    wide = 2 * V
    first_row = PADROWS + (64 if late else 0)
    if not late:
        phases[:, :, :PADROWS, :] = jnp.zeros((2, 2, PADROWS, PHASES * PB), jnp.float32)
    for n in range(2):
        arrival = SLOTS - 2 + n
        slot = info_ref[arrival]
        halves = tensors[2 * n : 2 * n + 2] if late else tensors[n : n + 1]
        blocks = [half[:, i * BLOCK : (i + 1) * BLOCK] for half in halves for i in range(2)]
        chunks = (1, 2, 3) if late else (0, 1)
        gather_some(info_ref[SLOTS + arrival], blocks, chunks, phases.at[n])
        term = None
        for j in range(TAPS):
            shifted = jnp.concatenate(
                [phases[n, c, first_row - j : first_row - j + rows, :] for c in range(2)], axis=0
            )
            product = lax.dot_general(
                shifted.astype(jnp.bfloat16),
                histories(slips, slot, j),
                (((1,), (1,)), ((), ())),
                preferred_element_type=jnp.float32,
            )
            term = product if term is None else term + product
        if n == 0:
            for c in range(2):
                low = c * BLOCK + (rows if late else 0)
                total[c * rows : (c + 1) * rows, :] = (
                    before[low : low + rows, :] + term[c * rows : (c + 1) * rows, :]
                )
        else:
            total[...] += term

    part = SPAN // PHASES
    spans = rows // part
    lane = lax.broadcasted_iota(jnp.int32, (part, wide), 1)
    for a in range(spans):
        for b in range(PHASES):
            half = slice((b // 2) * wide, (b // 2 + 1) * wide)
            first = total[a * part : (a + 1) * part, half]
            second = total[rows + a * part : rows + (a + 1) * part, half]
            if b % 2 == 0:
                second = pltpu.roll(second, V, 1)
            else:
                first = pltpu.roll(first, V, 1)
            traces[b * part : (b + 1) * part, a * wide : (a + 1) * wide] = jnp.where(
                lane < V, first, second
            ).astype(jnp.bfloat16)

    width = spans * wide
    nothing = jnp.zeros((SPAN, width), jnp.bfloat16)
    stacked[:SPAN, :] = traces[...]
    stacked[SPAN : 2 * SPAN, wide:] = traces[:, : width - wide]
    if late:
        stacked[SPAN : 2 * SPAN, :wide] = known[:, width - wide :]
        stacked[2 * SPAN : 3 * SPAN, :] = known[...]
        near = jnp.concatenate([known[:, 2 * wide :], traces[:, : 2 * wide]], axis=1)
        far = jnp.concatenate([known[:, wide:], traces[:, :wide]], axis=1)
        low = 0
    else:
        stacked[SPAN : 2 * SPAN, :wide] = nothing[:, :wide]
        stacked[2 * SPAN : 3 * SPAN, :] = nothing
        stacked[3 * SPAN :, : 2 * wide] = nothing[:, : 2 * wide]
        near = traces[:, : 2 * wide]
        far = jnp.concatenate([nothing[:, :wide], traces[:, :wide]], axis=1)
        low = 2 * wide
    states = jnp.dot(
        weights_ref[...],
        jnp.concatenate([near, far], axis=0),
        preferred_element_type=jnp.float32,
    )
    stacked[3 * SPAN :, low:] = states.astype(jnp.bfloat16)
    out_ref[...] = peaks[...] if late else jnp.zeros_like(out_ref)

    @pl.loop(0, NPER // QSTEP)
    def _(step):
        table = table_ref[pl.ds(step * QSTEP, QSTEP)].reshape(QSTEP * SPAN, 4 * SPAN)
        deep = 4 * SPAN if late else 2 * SPAN
        one = jnp.dot(
            table[:, :deep], stacked[:deep, : 2 * wide], preferred_element_type=jnp.float32
        )
        two = jnp.dot(table, stacked[:, 2 * wide :], preferred_element_type=jnp.float32)
        both = jnp.maximum(jnp.abs(one), jnp.abs(two))
        for n in range(QSTEP):
            highest = jnp.max(both[n * SPAN : (n + 1) * SPAN], axis=0, keepdims=True)
            highest = jnp.maximum(highest[:, :wide], highest[:, wide:])
            q = step * QSTEP + n
            owner, rank = place_ref[q], place_ref[NPER + q]
            if late:
                highest = jnp.maximum(highest, peaks[owner, pl.ds(rank, 1), :])
            out_ref[owner, pl.ds(rank, 1), :] = highest


def finish(late, info, place, tensors, slips, before, table, weights, known):
    smem = pl.BlockSpec(memory_space=pltpu.SMEM)
    vmem = pl.BlockSpec(memory_space=pltpu.VMEM)
    operands = [*tensors, slips, before, table, weights, *known]
    out_shape = [jax.ShapeDtypeStruct((OWNERS, PMAX, 2 * V), jnp.float32)]
    traces = (SPAN, HALF // SPAN * 2 * V)
    scratch = []
    if late:
        scratch = [pltpu.VMEM(traces, jnp.bfloat16)]
    else:
        out_shape.append(jax.ShapeDtypeStruct(traces, jnp.bfloat16))
    held = PADROWS + (192 if late else 128)
    return pl.pallas_call(
        functools.partial(finish_kernel, late),
        out_shape=out_shape,
        in_specs=[smem, smem] + [vmem] * len(operands),
        out_specs=[vmem] * len(out_shape),
        scratch_shapes=scratch
        + [
            pltpu.VMEM((2, 2, held, PHASES * PB), jnp.float32),
            pltpu.VMEM((BLOCK, PHASES * V), jnp.float32),
            pltpu.VMEM((4 * SPAN, HALF // SPAN * 2 * V), jnp.bfloat16),
        ],
        compiler_params=pltpu.CompilerParams(vmem_limit_bytes=LARGE),
        cost_estimate=pl.CostEstimate(
            flops=3600000000, bytes_accessed=8000000, transcendentals=0
        ),
        name="finish",
    )(info, place, *operands)


def send(block, n):
    pairs = [(g, target(g, *STEPS[n])) for g in range(SLOTS)]
    return lax.ppermute(block, "sgt", pairs)


def local(
    sgt_tensor, moment, slip_rate, footprint, live_blocks, start_delay, frequency, period_owner
):
    here = lax.axis_index("sgt")
    rupture = here * OWNERS + lax.axis_index("work")
    outgoing = list(project(STEPS, footprint, sgt_tensor, moment))
    tensors = [outgoing[0]]
    for n in range(1, SLOTS - 2):
        tensors.append(send(outgoing[n], n))
    first, second = SLOTS - 2, SLOTS - 1
    halves = {first: [], second: []}

    def send_after(part, n, arrived):
        block, tensors[arrived] = lax.optimization_barrier((outgoing[part], tensors[arrived]))
        halves[n].append(send(block, n))

    send_after(SLOTS - 2, first, 1)
    send_after(SLOTS, second, 2)
    slip_rate, frequency, tensors[1] = lax.optimization_barrier(
        (slip_rate, frequency, tensors[1])
    )
    own_blocks = lax.dynamic_index_in_dim(footprint, rupture, 0, keepdims=False)
    own_count = lax.dynamic_index_in_dim(live_blocks, rupture, 0, keepdims=False)
    own_delays = lax.dynamic_index_in_dim(start_delay, rupture, 0, keepdims=False)
    origins = jnp.stack([origin(here, dz, dc) for dz, dc in STEPS])
    match = (own_blocks >> 2)[None, :] == origins[:, None]
    slot = jnp.sum(jnp.where(match, jnp.arange(SLOTS)[None, :], 0), axis=1)
    delay = jnp.sum(jnp.where(match, own_delays[None, :], 0), axis=1)
    info = jnp.concatenate([slot, jnp.where(slot < own_count, delay, 4 * NT)])

    slips = jnp.transpose(slip_rate[0], (0, 3, 1, 2)).reshape(SLOTS, L * V, PB)
    table, weights = tables(frequency)
    period_ids = jnp.arange(NPER)
    same_owner = period_owner[:, None] == period_owner[None, :]
    earlier = period_ids[None, :] < period_ids[:, None]
    rank = jnp.sum(same_owner & earlier, axis=1).astype(jnp.int32)
    place = jnp.concatenate([period_owner, rank])

    running = None
    for n, arrivals in enumerate(GROUPS):
        running = convolve(arrivals, info, [tensors[n] for n in arrivals], slips, running)
        if n == 1:
            outgoing[SLOTS - 1], outgoing[SLOTS + 1], running, table = lax.optimization_barrier(
                (outgoing[SLOTS - 1], outgoing[SLOTS + 1], running, table)
            )
            send_after(SLOTS - 1, first, 4)
            send_after(SLOTS + 1, second, 5)
    peaks, known = finish(
        False,
        info,
        place,
        [halves[first][0], halves[second][0]],
        slips,
        running,
        table,
        weights,
        [],
    )
    (peaks,) = finish(
        True,
        info,
        place,
        halves[first] + halves[second],
        slips,
        running,
        table,
        weights,
        [known, peaks],
    )
    peaks = lax.all_to_all(peaks, "work", split_axis=0, concat_axis=0, tiled=True)
    result = jnp.transpose(peaks.reshape(OWNERS, PMAX, 2, V), (1, 2, 0, 3))
    return result[None]


def solution(mesh):
    in_specs = (
        P("sgt", None, None, None, None),
        P("sgt", None, None),
        P(("sgt", "work"), None, None, None, None),
        P(),
        P(),
        P(),
        P(),
        P(),
    )
    out_specs = P("work", None, None, "sgt", None)
    return jax.shard_map(local, mesh=mesh, in_specs=in_specs, out_specs=out_specs, check_vma=False)
```

```python
import functools
import math

import jax
import jax.numpy as jnp
from jax import lax
from jax.experimental import pallas as pl
from jax.experimental.pallas import tpu as pltpu
from jax.sharding import PartitionSpec as P

NT = 1024
L = 32
KIR = 512
V = 64
PB = 128
NPER = 44
SLOTS = 8
HELD = 4
NJ = 6
PMAX = 3
OWNERS = 16
damping = 0.05

PHASES = 4
TAPS = 9
PADROWS = 16
BLOCK = 256
HALF = NT // 2
SPAN = 128
AHEAD = 4
TSTEP = 4
QSTEP = 22
SMALL = 12 * 1024 * 1024
LARGE = 28 * 1024 * 1024
PROJECT = 60 * 1024 * 1024

STEPS = ((0, 0), (0, 1), (2, 0), (2, 1), (1, 0), (3, 0), (1, 1), (3, 1))
GROUPS = ((0, 1), (2, 3), (4, 5))


def target(place, dz, dc):
    return ((place + 2 * dz) & 7) ^ dc


def origin(place, dz, dc):
    return ((place - 2 * dz) & 7) ^ dc


def project_block(weights, taken, scr, c):
    for i in range(0, PB, 16):
        total = None
        for j in range(NJ):
            term = weights[i : i + 16, j : j + 1] * taken[j, c, i : i + 16, :].astype(jnp.float32)
            total = term if total is None else total + term
        scr[c * PB + i : c * PB + i + 16, :] = total.astype(jnp.bfloat16)


def pieces(steps):
    parts = []
    for n in range(len(steps)):
        if n < len(steps) - 2:
            parts.append((n, slice(0, NT)))
        else:
            parts += [(n, slice(0, HALF)), (n, slice(HALF, NT))]
    return parts


def project_kernel(steps, fp_ref, sgt_ref, mom_ref, *rest):
    parts = pieces(steps)
    outs, rest = rest[: len(parts)], rest[len(parts) :]
    taken, scr, table, chosen, moments, in_sem, out_sem, small_sem = rest
    fetch_table = pltpu.make_async_copy(fp_ref, table, small_sem.at[0])
    fetch_moments = pltpu.make_async_copy(mom_ref, moments, small_sem.at[1])
    fetch_moments.start()
    fetch_table.start()
    me = lax.axis_index("sgt")
    work = lax.axis_index("work")

    def load(n, c):
        return pltpu.make_async_copy(
            sgt_ref.at[n, :, c], taken.at[n, :, c], in_sem.at[2 * n + c]
        )

    for n in range(AHEAD // 2):
        for c in range(2):
            load(n, c).start()
    fetch_moments.wait()

    @pl.loop(0, HELD)
    def _(n):
        weights = jnp.transpose(
            jnp.concatenate([moments[j, pl.ds(n, 1), :] for j in range(NJ)], axis=0)
        )
        for c in range(2):
            load(n, c).wait()
            pl.when(n + AHEAD // 2 < HELD)(load(n + AHEAD // 2, c).start)
            project_block(weights, taken.at[n], scr.at[n], c)

        @pl.when(n == 0)
        def _():
            fetch_table.wait()
            for m, (dz, dc) in enumerate(steps):
                rupture = target(me, dz, dc) * OWNERS + work
                found = jnp.int32(0)
                for k in range(SLOTS):
                    block = table[k, rupture]
                    found = jnp.where((block >> 2) == me, block & 3, found)
                chosen[m] = found

        for m, (step, span) in enumerate(parts):
            copy = pltpu.make_async_copy(scr.at[n, :, span], outs[m], out_sem.at[m])
            pl.when(chosen[step] == n)(copy.start)

    for m, (step, span) in enumerate(parts):
        pltpu.make_async_copy(scr.at[0, :, span], outs[m], out_sem.at[m]).wait()


def project(steps, footprint, sgt_tensor, moment):
    parts = pieces(steps)
    return pl.pallas_call(
        functools.partial(project_kernel, steps),
        out_shape=[
            jax.ShapeDtypeStruct((2 * PB, span.stop - span.start), jnp.bfloat16) for _, span in parts
        ],
        in_specs=[
            pl.BlockSpec(memory_space=pl.ANY),
            pl.BlockSpec(memory_space=pl.ANY),
            pl.BlockSpec(memory_space=pl.ANY),
        ],
        out_specs=[pl.BlockSpec(memory_space=pl.ANY)] * len(parts),
        scratch_shapes=[
            pltpu.VMEM((HELD, NJ, 2, PB, NT), jnp.bfloat16),
            pltpu.VMEM((HELD, 2 * PB, NT), jnp.bfloat16),
            pltpu.SMEM((SLOTS, 128), jnp.int32),
            pltpu.SMEM((SLOTS,), jnp.int32),
            pltpu.VMEM((NJ, HELD, PB), jnp.float32),
            pltpu.SemaphoreType.DMA((2 * HELD,)),
            pltpu.SemaphoreType.DMA((len(parts),)),
            pltpu.SemaphoreType.DMA((2,)),
        ],
        compiler_params=pltpu.CompilerParams(vmem_limit_bytes=PROJECT),
        cost_estimate=pl.CostEstimate(
            flops=HELD * 100000000, bytes_accessed=HELD * 3200000, transcendentals=0
        ),
        name="project",
    )(footprint.T, sgt_tensor, jnp.transpose(moment, (1, 0, 2)))


def tables_kernel(u_ref, v_ref, out_ref):
    step = pl.program_id(0)
    columns = jnp.transpose(u_ref[0])
    row = lax.broadcasted_iota(jnp.int32, (SPAN, SPAN), 0)
    lane = lax.broadcasted_iota(jnp.int32, (SPAN, SPAN), 1)
    source = ((lane & 31) << 2) + (lane >> 5)
    for n in range(TSTEP):
        sine = columns[:, 2 * n : 2 * n + 1]
        cosine = columns[:, 2 * n + 1 : 2 * n + 2]
        for j in range(3):
            span = slice(j * SPAN, (j + 1) * SPAN)
            value = sine * v_ref[0, 2 * n : 2 * n + 1, span] + (
                cosine * v_ref[0, 2 * n + 1 : 2 * n + 2, span]
            )
            if j == 0:
                value = jnp.where(row >= source, value, 0.0)
            if j == 2:
                value = jnp.where(row < source, value, 0.0)
            out_ref[n, :, span] = value.astype(jnp.bfloat16)
        state = 2 * (step * TSTEP + n)
        value = jnp.where(lane == state, sine, 0.0) + jnp.where(lane == state + 1, cosine, 0.0)
        out_ref[n, :, 3 * SPAN :] = value.astype(jnp.bfloat16)


def tables(frequency):
    angular = frequency[:, None]
    damped = angular * math.sqrt(1.0 - damping * damping)
    rows = jnp.arange(SPAN, dtype=jnp.float32)[None, :]
    decay = jnp.exp(-damping * angular * rows)
    u = jnp.stack([decay * jnp.sin(damped * rows), decay * jnp.cos(damped * rows)], axis=1)
    lane = jnp.arange(5 * SPAN)
    inner = lane % SPAN
    source = ((inner & 31) << 2) + (inner >> 5)
    before = jnp.asarray([0, 1, 4, 2, 3])[lane // SPAN]
    back = (source - before * SPAN).astype(jnp.float32)[None, :]
    growth = angular * angular / damped * jnp.exp(damping * angular * back)
    v = jnp.stack([growth * jnp.cos(damped * back), -growth * jnp.sin(damped * back)], axis=1)
    weights = v[..., 3 * SPAN :].reshape(2 * NPER, 2 * SPAN)
    weights = jnp.pad(weights, ((0, SPAN - 2 * NPER), (0, 0))).astype(jnp.bfloat16)
    steps = NPER // TSTEP
    table = pl.pallas_call(
        tables_kernel,
        out_shape=jax.ShapeDtypeStruct((NPER, SPAN, 4 * SPAN), jnp.bfloat16),
        grid=(steps,),
        in_specs=[
            pl.BlockSpec((1, 2 * TSTEP, SPAN), lambda s: (s, 0, 0)),
            pl.BlockSpec((1, 2 * TSTEP, 3 * SPAN), lambda s: (s, 0, 0)),
        ],
        out_specs=pl.BlockSpec((TSTEP, SPAN, 4 * SPAN), lambda s: (s, 0, 0)),
        compiler_params=pltpu.CompilerParams(vmem_limit_bytes=SMALL),
        cost_estimate=pl.CostEstimate(
            flops=NPER * 4 * SPAN * SPAN * 5, bytes_accessed=6000000, transcendentals=0
        ),
        name="tables",
    )(u.reshape(steps, 2 * TSTEP, SPAN), v[..., : 3 * SPAN].reshape(steps, 2 * TSTEP, 3 * SPAN))
    return table, weights


def gather_phases(delay, tensor_ref, phases):
    rows = lax.broadcasted_iota(jnp.int32, (BLOCK, 2 * BLOCK), 0)
    lane = lax.broadcasted_iota(jnp.int32, (BLOCK, 2 * BLOCK), 1)
    part = BLOCK // PHASES
    source = BLOCK + ((rows & 63) << 2) + (rows >> 6) - delay
    pick = jnp.where(lane == source, 1.0, 0.0).astype(jnp.bfloat16)
    for a in range(NT // BLOCK):
        low = max(a - 1, 0) * BLOCK
        window = tensor_ref[:, low : (a + 1) * BLOCK]
        chosen = pick[:, 2 * BLOCK - window.shape[1] :]
        moved = lax.dot_general(
            chosen, window, (((1,), (1,)), ((), ())), preferred_element_type=jnp.float32
        )
        for c in range(2):
            for b in range(PHASES):
                phases[
                    c, PADROWS + a * part : PADROWS + (a + 1) * part, b * PB : (b + 1) * PB
                ] = moved[b * part : (b + 1) * part, c * PB : (c + 1) * PB]


def histories(slips, slot, shift):
    pieces = []
    for b in range(PHASES):
        first = PHASES * shift - b
        low, high = max(first, 0), min(first + PHASES, L)
        if high <= low:
            pieces.append(jnp.zeros((PHASES * V, PB), jnp.bfloat16))
            continue
        parts = [slips[slot, low * V : high * V, :]]
        if low > first:
            parts.insert(0, jnp.zeros(((low - first) * V, PB), jnp.bfloat16))
        if high < first + PHASES:
            parts.append(jnp.zeros(((first + PHASES - high) * V, PB), jnp.bfloat16))
        pieces.append(parts[0] if len(parts) == 1 else jnp.concatenate(parts, axis=0))
    return jnp.concatenate(pieces, axis=1)


def convolve_kernel(arrivals, begins, info_ref, *rest):
    count = len(arrivals)
    tensors, slips, rest = rest[:count], rest[count], rest[count + 1 :]
    before = None
    if not begins:
        before, rest = rest[0], rest[1:]
    out_ref, phases = rest
    for half in range(2):
        phases[half, :, :PADROWS, :] = jnp.zeros((2, PADROWS, PHASES * PB), jnp.float32)
    for n in range(count):
        half = n % 2
        slot = info_ref[arrivals[n]]
        gather_phases(info_ref[SLOTS + arrivals[n]], tensors[n], phases.at[half])
        for c in range(2):
            rows = slice(c * BLOCK, (c + 1) * BLOCK)
            term = None
            for j in range(TAPS):
                shifted = phases[half, c, PADROWS - j : PADROWS - j + BLOCK, :]
                product = lax.dot_general(
                    shifted.astype(jnp.bfloat16),
                    histories(slips, slot, j),
                    (((1,), (1,)), ((), ())),
                    preferred_element_type=jnp.float32,
                )
                term = product if term is None else term + product
            if n > 0:
                out_ref[rows, :] += term
            elif begins:
                out_ref[rows, :] = term
            else:
                out_ref[rows, :] = before[rows, :] + term


def convolve(arrivals, info, tensors, slips, before):
    count = len(arrivals)
    vmem = pl.BlockSpec(memory_space=pltpu.VMEM)
    begins = before is None
    return pl.pallas_call(
        functools.partial(convolve_kernel, arrivals, begins),
        out_shape=jax.ShapeDtypeStruct((2 * BLOCK, PHASES * V), jnp.float32),
        in_specs=[pl.BlockSpec(memory_space=pltpu.SMEM)]
        + [vmem] * (count + 1)
        + ([] if begins else [vmem]),
        out_specs=vmem,
        scratch_shapes=[
            pltpu.VMEM((2, 2, PADROWS + BLOCK, PHASES * PB), jnp.float32),
        ],
        compiler_params=pltpu.CompilerParams(vmem_limit_bytes=LARGE),
        cost_estimate=pl.CostEstimate(
            flops=count * 1800000000, bytes_accessed=count * 1048576, transcendentals=0
        ),
        name="convolve",
    )(info, *tensors, slips, *([] if begins else [before]))


def pick_phases(delay):
    rows = lax.broadcasted_iota(jnp.int32, (BLOCK, 2 * BLOCK), 0)
    lane = lax.broadcasted_iota(jnp.int32, (BLOCK, 2 * BLOCK), 1)
    source = BLOCK + ((rows & 63) << 2) + (rows >> 6) - delay
    return jnp.where(lane == source, 1.0, 0.0).astype(jnp.bfloat16)


def gather_some(delay, blocks, chunks, phases):
    pick = pick_phases(delay)
    part = BLOCK // PHASES
    dims = (((1,), (1,)), ((), ()))
    for place, a in enumerate(chunks):
        moved = lax.dot_general(
            pick[:, BLOCK:], blocks[a], dims, preferred_element_type=jnp.float32
        )
        if a > 0:
            moved += lax.dot_general(
                pick[:, :BLOCK], blocks[a - 1], dims, preferred_element_type=jnp.float32
            )
        low = PADROWS + place * part
        for c in range(2):
            for b in range(PHASES):
                phases[c, low : low + part, b * PB : (b + 1) * PB] = moved[
                    b * part : (b + 1) * part, c * PB : (c + 1) * PB
                ]


def finish_kernel(late, info_ref, place_ref, *rest):
    count = 4 if late else 2
    tensors, rest = rest[:count], rest[count:]
    slips, before, table_ref, weights_ref = rest[:4]
    rest = rest[4:]
    known, peaks = None, None
    if late:
        known, peaks = rest[:2]
        rest = rest[2:]
    out_ref, traces = rest[0], rest[1]
    phases, total, stacked = rest[2:]
    rows = BLOCK // 2
    wide = 2 * V
    first_row = PADROWS + (64 if late else 0)
    if not late:
        phases[:, :, :PADROWS, :] = jnp.zeros((2, 2, PADROWS, PHASES * PB), jnp.float32)
    for n in range(2):
        arrival = SLOTS - 2 + n
        slot = info_ref[arrival]
        halves = tensors[2 * n : 2 * n + 2] if late else tensors[n : n + 1]
        blocks = [half[:, i * BLOCK : (i + 1) * BLOCK] for half in halves for i in range(2)]
        chunks = (1, 2, 3) if late else (0, 1)
        gather_some(info_ref[SLOTS + arrival], blocks, chunks, phases.at[n])
        term = None
        for j in range(TAPS):
            shifted = jnp.concatenate(
                [phases[n, c, first_row - j : first_row - j + rows, :] for c in range(2)], axis=0
            )
            product = lax.dot_general(
                shifted.astype(jnp.bfloat16),
                histories(slips, slot, j),
                (((1,), (1,)), ((), ())),
                preferred_element_type=jnp.float32,
            )
            term = product if term is None else term + product
        if n == 0:
            for c in range(2):
                low = c * BLOCK + (rows if late else 0)
                total[c * rows : (c + 1) * rows, :] = (
                    before[low : low + rows, :] + term[c * rows : (c + 1) * rows, :]
                )
        else:
            total[...] += term

    part = SPAN // PHASES
    spans = rows // part
    lane = lax.broadcasted_iota(jnp.int32, (part, wide), 1)
    for a in range(spans):
        for b in range(PHASES):
            half = slice((b // 2) * wide, (b // 2 + 1) * wide)
            first = total[a * part : (a + 1) * part, half]
            second = total[rows + a * part : rows + (a + 1) * part, half]
            if b % 2 == 0:
                second = pltpu.roll(second, V, 1)
            else:
                first = pltpu.roll(first, V, 1)
            traces[b * part : (b + 1) * part, a * wide : (a + 1) * wide] = jnp.where(
                lane < V, first, second
            ).astype(jnp.bfloat16)

    width = spans * wide
    nothing = jnp.zeros((SPAN, width), jnp.bfloat16)
    stacked[:SPAN, :] = traces[...]
    stacked[SPAN : 2 * SPAN, wide:] = traces[:, : width - wide]
    if late:
        stacked[SPAN : 2 * SPAN, :wide] = known[:, width - wide :]
        stacked[2 * SPAN : 3 * SPAN, :] = known[...]
        near = jnp.concatenate([known[:, 2 * wide :], traces[:, : 2 * wide]], axis=1)
        far = jnp.concatenate([known[:, wide:], traces[:, :wide]], axis=1)
        low = 0
    else:
        stacked[SPAN : 2 * SPAN, :wide] = nothing[:, :wide]
        stacked[2 * SPAN : 3 * SPAN, :] = nothing
        stacked[3 * SPAN :, : 2 * wide] = nothing[:, : 2 * wide]
        near = traces[:, : 2 * wide]
        far = jnp.concatenate([nothing[:, :wide], traces[:, :wide]], axis=1)
        low = 2 * wide
    states = jnp.dot(
        weights_ref[...],
        jnp.concatenate([near, far], axis=0),
        preferred_element_type=jnp.float32,
    )
    stacked[3 * SPAN :, low:] = states.astype(jnp.bfloat16)
    out_ref[...] = peaks[...] if late else jnp.zeros_like(out_ref)

    @pl.loop(0, NPER // QSTEP)
    def _(step):
        table = table_ref[pl.ds(step * QSTEP, QSTEP)].reshape(QSTEP * SPAN, 4 * SPAN)
        deep = 4 * SPAN if late else 2 * SPAN
        one = jnp.dot(
            table[:, :deep], stacked[:deep, : 2 * wide], preferred_element_type=jnp.float32
        )
        two = jnp.dot(table, stacked[:, 2 * wide :], preferred_element_type=jnp.float32)
        both = jnp.maximum(jnp.abs(one), jnp.abs(two))
        for n in range(QSTEP):
            highest = jnp.max(both[n * SPAN : (n + 1) * SPAN], axis=0, keepdims=True)
            highest = jnp.maximum(highest[:, :wide], highest[:, wide:])
            q = step * QSTEP + n
            owner, rank = place_ref[q], place_ref[NPER + q]
            if late:
                highest = jnp.maximum(highest, peaks[owner, pl.ds(rank, 1), :])
            out_ref[owner, pl.ds(rank, 1), :] = highest


def finish(late, info, place, tensors, slips, before, table, weights, known):
    smem = pl.BlockSpec(memory_space=pltpu.SMEM)
    vmem = pl.BlockSpec(memory_space=pltpu.VMEM)
    operands = [*tensors, slips, before, table, weights, *known]
    out_shape = [jax.ShapeDtypeStruct((OWNERS, PMAX, 2 * V), jnp.float32)]
    traces = (SPAN, HALF // SPAN * 2 * V)
    scratch = []
    if late:
        scratch = [pltpu.VMEM(traces, jnp.bfloat16)]
    else:
        out_shape.append(jax.ShapeDtypeStruct(traces, jnp.bfloat16))
    held = PADROWS + (192 if late else 128)
    return pl.pallas_call(
        functools.partial(finish_kernel, late),
        out_shape=out_shape,
        in_specs=[smem, smem] + [vmem] * len(operands),
        out_specs=[vmem] * len(out_shape),
        scratch_shapes=scratch
        + [
            pltpu.VMEM((2, 2, held, PHASES * PB), jnp.float32),
            pltpu.VMEM((BLOCK, PHASES * V), jnp.float32),
            pltpu.VMEM((4 * SPAN, HALF // SPAN * 2 * V), jnp.bfloat16),
        ],
        compiler_params=pltpu.CompilerParams(vmem_limit_bytes=LARGE),
        cost_estimate=pl.CostEstimate(
            flops=3600000000, bytes_accessed=8000000, transcendentals=0
        ),
        name="finish",
    )(info, place, *operands)


def send(block, n):
    pairs = [(g, target(g, *STEPS[n])) for g in range(SLOTS)]
    return lax.ppermute(block, "sgt", pairs)


def local(
    sgt_tensor, moment, slip_rate, footprint, live_blocks, start_delay, frequency, period_owner
):
    here = lax.axis_index("sgt")
    rupture = here * OWNERS + lax.axis_index("work")
    outgoing = list(project(STEPS, footprint, sgt_tensor, moment))
    tensors = [outgoing[0]]
    for n in range(1, SLOTS - 2):
        tensors.append(send(outgoing[n], n))
    first, second = SLOTS - 2, SLOTS - 1
    halves = {first: [], second: []}

    def send_after(part, n, arrived):
        block, tensors[arrived] = lax.optimization_barrier((outgoing[part], tensors[arrived]))
        halves[n].append(send(block, n))

    send_after(SLOTS - 2, first, 1)
    send_after(SLOTS, second, 2)
    slip_rate, frequency, tensors[1] = lax.optimization_barrier(
        (slip_rate, frequency, tensors[1])
    )
    own_blocks = lax.dynamic_index_in_dim(footprint, rupture, 0, keepdims=False)
    own_count = lax.dynamic_index_in_dim(live_blocks, rupture, 0, keepdims=False)
    own_delays = lax.dynamic_index_in_dim(start_delay, rupture, 0, keepdims=False)
    origins = jnp.stack([origin(here, dz, dc) for dz, dc in STEPS])
    match = (own_blocks >> 2)[None, :] == origins[:, None]
    slot = jnp.sum(jnp.where(match, jnp.arange(SLOTS)[None, :], 0), axis=1)
    delay = jnp.sum(jnp.where(match, own_delays[None, :], 0), axis=1)
    info = jnp.concatenate([slot, jnp.where(slot < own_count, delay, 4 * NT)])

    slips = jnp.transpose(slip_rate[0], (0, 3, 1, 2)).reshape(SLOTS, L * V, PB)
    table, weights = tables(frequency)
    period_ids = jnp.arange(NPER)
    same_owner = period_owner[:, None] == period_owner[None, :]
    earlier = period_ids[None, :] < period_ids[:, None]
    rank = jnp.sum(same_owner & earlier, axis=1).astype(jnp.int32)
    place = jnp.concatenate([period_owner, rank])

    running = None
    for n, arrivals in enumerate(GROUPS):
        running = convolve(arrivals, info, [tensors[n] for n in arrivals], slips, running)
        if n == 1:
            outgoing[SLOTS - 1], outgoing[SLOTS + 1], running, table = lax.optimization_barrier(
                (outgoing[SLOTS - 1], outgoing[SLOTS + 1], running, table)
            )
            send_after(SLOTS - 1, first, 4)
            send_after(SLOTS + 1, second, 5)
    peaks, known = finish(
        False,
        info,
        place,
        [halves[first][0], halves[second][0]],
        slips,
        running,
        table,
        weights,
        [],
    )
    (peaks,) = finish(
        True,
        info,
        place,
        halves[first] + halves[second],
        slips,
        running,
        table,
        weights,
        [known, peaks],
    )
    peaks = lax.all_to_all(peaks, "work", split_axis=0, concat_axis=0, tiled=True)
    result = jnp.transpose(peaks.reshape(OWNERS, PMAX, 2, V), (1, 2, 0, 3))
    return result[None]


def solution(mesh):
    in_specs = (
        P("sgt", None, None, None, None),
        P("sgt", None, None),
        P(("sgt", "work"), None, None, None, None),
        P(),
        P(),
        P(),
        P(),
        P(),
    )
    out_specs = P("work", None, None, "sgt", None)
    return jax.shard_map(local, mesh=mesh, in_specs=in_specs, out_specs=out_specs, check_vma=False)
```

```python
import functools
import math

import jax
import jax.numpy as jnp
from jax import lax
from jax.experimental import pallas as pl
from jax.experimental.pallas import tpu as pltpu
from jax.sharding import PartitionSpec as P

NT = 1024
L = 32
KIR = 512
V = 64
PB = 128
NPER = 44
SLOTS = 8
HELD = 4
NJ = 6
PMAX = 3
OWNERS = 16
damping = 0.05

PHASES = 4
TAPS = 9
PADROWS = 16
BLOCK = 256
HALF = NT // 2
SPAN = 128
AHEAD = 6
TSTEP = 4
QSTEP = 22
SMALL = 12 * 1024 * 1024
LARGE = 28 * 1024 * 1024
PROJECT = 60 * 1024 * 1024

STEPS = ((0, 0), (0, 1), (2, 0), (2, 1), (1, 0), (3, 0), (1, 1), (3, 1))
GROUPS = ((0, 1), (2, 3), (4, 5))


def target(place, dz, dc):
    return ((place + 2 * dz) & 7) ^ dc


def origin(place, dz, dc):
    return ((place - 2 * dz) & 7) ^ dc


def project_block(weights, taken, scr, c):
    for i in range(0, PB, 16):
        total = None
        for j in range(NJ):
            term = weights[i : i + 16, j : j + 1] * taken[j, c, i : i + 16, :].astype(jnp.float32)
            total = term if total is None else total + term
        scr[c * PB + i : c * PB + i + 16, :] = total.astype(jnp.bfloat16)


def pieces(steps):
    parts = []
    for n in range(len(steps)):
        if n < len(steps) - 2:
            parts.append((n, slice(0, NT)))
        else:
            parts += [(n, slice(0, HALF)), (n, slice(HALF, NT))]
    return parts


def project_kernel(steps, fp_ref, sgt_ref, mom_ref, *rest):
    parts = pieces(steps)
    outs, rest = rest[: len(parts)], rest[len(parts) :]
    taken, scr, table, chosen, moments, in_sem, out_sem, small_sem = rest
    fetch_table = pltpu.make_async_copy(fp_ref, table, small_sem.at[0])
    fetch_moments = pltpu.make_async_copy(mom_ref, moments, small_sem.at[1])
    fetch_moments.start()
    fetch_table.start()
    me = lax.axis_index("sgt")
    work = lax.axis_index("work")

    def load(n, c):
        return pltpu.make_async_copy(
            sgt_ref.at[n, :, c], taken.at[n, :, c], in_sem.at[2 * n + c]
        )

    for n in range(AHEAD // 2):
        for c in range(2):
            load(n, c).start()
    fetch_moments.wait()

    @pl.loop(0, HELD)
    def _(n):
        weights = jnp.transpose(
            jnp.concatenate([moments[j, pl.ds(n, 1), :] for j in range(NJ)], axis=0)
        )
        for c in range(2):
            load(n, c).wait()
            pl.when(n + AHEAD // 2 < HELD)(load(n + AHEAD // 2, c).start)
            project_block(weights, taken.at[n], scr.at[n], c)

        @pl.when(n == 0)
        def _():
            fetch_table.wait()
            for m, (dz, dc) in enumerate(steps):
                rupture = target(me, dz, dc) * OWNERS + work
                found = jnp.int32(0)
                for k in range(SLOTS):
                    block = table[k, rupture]
                    found = jnp.where((block >> 2) == me, block & 3, found)
                chosen[m] = found

        for m, (step, span) in enumerate(parts):
            copy = pltpu.make_async_copy(scr.at[n, :, span], outs[m], out_sem.at[m])
            pl.when(chosen[step] == n)(copy.start)

    for m, (step, span) in enumerate(parts):
        pltpu.make_async_copy(scr.at[0, :, span], outs[m], out_sem.at[m]).wait()


def project(steps, footprint, sgt_tensor, moment):
    parts = pieces(steps)
    return pl.pallas_call(
        functools.partial(project_kernel, steps),
        out_shape=[
            jax.ShapeDtypeStruct((2 * PB, span.stop - span.start), jnp.bfloat16) for _, span in parts
        ],
        in_specs=[
            pl.BlockSpec(memory_space=pl.ANY),
            pl.BlockSpec(memory_space=pl.ANY),
            pl.BlockSpec(memory_space=pl.ANY),
        ],
        out_specs=[pl.BlockSpec(memory_space=pl.ANY)] * len(parts),
        scratch_shapes=[
            pltpu.VMEM((HELD, NJ, 2, PB, NT), jnp.bfloat16),
            pltpu.VMEM((HELD, 2 * PB, NT), jnp.bfloat16),
            pltpu.SMEM((SLOTS, 128), jnp.int32),
            pltpu.SMEM((SLOTS,), jnp.int32),
            pltpu.VMEM((NJ, HELD, PB), jnp.float32),
            pltpu.SemaphoreType.DMA((2 * HELD,)),
            pltpu.SemaphoreType.DMA((len(parts),)),
            pltpu.SemaphoreType.DMA((2,)),
        ],
        compiler_params=pltpu.CompilerParams(vmem_limit_bytes=PROJECT),
        cost_estimate=pl.CostEstimate(
            flops=HELD * 100000000, bytes_accessed=HELD * 3200000, transcendentals=0
        ),
        name="project",
    )(footprint.T, sgt_tensor, jnp.transpose(moment, (1, 0, 2)))


def tables_kernel(u_ref, v_ref, out_ref):
    step = pl.program_id(0)
    columns = jnp.transpose(u_ref[0])
    row = lax.broadcasted_iota(jnp.int32, (SPAN, SPAN), 0)
    lane = lax.broadcasted_iota(jnp.int32, (SPAN, SPAN), 1)
    source = ((lane & 31) << 2) + (lane >> 5)
    for n in range(TSTEP):
        sine = columns[:, 2 * n : 2 * n + 1]
        cosine = columns[:, 2 * n + 1 : 2 * n + 2]
        for j in range(3):
            span = slice(j * SPAN, (j + 1) * SPAN)
            value = sine * v_ref[0, 2 * n : 2 * n + 1, span] + (
                cosine * v_ref[0, 2 * n + 1 : 2 * n + 2, span]
            )
            if j == 0:
                value = jnp.where(row >= source, value, 0.0)
            if j == 2:
                value = jnp.where(row < source, value, 0.0)
            out_ref[n, :, span] = value.astype(jnp.bfloat16)
        state = 2 * (step * TSTEP + n)
        value = jnp.where(lane == state, sine, 0.0) + jnp.where(lane == state + 1, cosine, 0.0)
        out_ref[n, :, 3 * SPAN :] = value.astype(jnp.bfloat16)


def tables(frequency):
    angular = frequency[:, None]
    damped = angular * math.sqrt(1.0 - damping * damping)
    rows = jnp.arange(SPAN, dtype=jnp.float32)[None, :]
    decay = jnp.exp(-damping * angular * rows)
    u = jnp.stack([decay * jnp.sin(damped * rows), decay * jnp.cos(damped * rows)], axis=1)
    lane = jnp.arange(5 * SPAN)
    inner = lane % SPAN
    source = ((inner & 31) << 2) + (inner >> 5)
    before = jnp.asarray([0, 1, 4, 2, 3])[lane // SPAN]
    back = (source - before * SPAN).astype(jnp.float32)[None, :]
    growth = angular * angular / damped * jnp.exp(damping * angular * back)
    v = jnp.stack([growth * jnp.cos(damped * back), -growth * jnp.sin(damped * back)], axis=1)
    weights = v[..., 3 * SPAN :].reshape(2 * NPER, 2 * SPAN)
    weights = jnp.pad(weights, ((0, SPAN - 2 * NPER), (0, 0))).astype(jnp.bfloat16)
    steps = NPER // TSTEP
    table = pl.pallas_call(
        tables_kernel,
        out_shape=jax.ShapeDtypeStruct((NPER, SPAN, 4 * SPAN), jnp.bfloat16),
        grid=(steps,),
        in_specs=[
            pl.BlockSpec((1, 2 * TSTEP, SPAN), lambda s: (s, 0, 0)),
            pl.BlockSpec((1, 2 * TSTEP, 3 * SPAN), lambda s: (s, 0, 0)),
        ],
        out_specs=pl.BlockSpec((TSTEP, SPAN, 4 * SPAN), lambda s: (s, 0, 0)),
        compiler_params=pltpu.CompilerParams(vmem_limit_bytes=SMALL),
        cost_estimate=pl.CostEstimate(
            flops=NPER * 4 * SPAN * SPAN * 5, bytes_accessed=6000000, transcendentals=0
        ),
        name="tables",
    )(u.reshape(steps, 2 * TSTEP, SPAN), v[..., : 3 * SPAN].reshape(steps, 2 * TSTEP, 3 * SPAN))
    return table, weights


def gather_phases(delay, tensor_ref, phases):
    rows = lax.broadcasted_iota(jnp.int32, (BLOCK, 2 * BLOCK), 0)
    lane = lax.broadcasted_iota(jnp.int32, (BLOCK, 2 * BLOCK), 1)
    part = BLOCK // PHASES
    source = BLOCK + ((rows & 63) << 2) + (rows >> 6) - delay
    pick = jnp.where(lane == source, 1.0, 0.0).astype(jnp.bfloat16)
    for a in range(NT // BLOCK):
        low = max(a - 1, 0) * BLOCK
        window = tensor_ref[:, low : (a + 1) * BLOCK]
        chosen = pick[:, 2 * BLOCK - window.shape[1] :]
        moved = lax.dot_general(
            chosen, window, (((1,), (1,)), ((), ())), preferred_element_type=jnp.float32
        )
        for c in range(2):
            for b in range(PHASES):
                phases[
                    c, PADROWS + a * part : PADROWS + (a + 1) * part, b * PB : (b + 1) * PB
                ] = moved[b * part : (b + 1) * part, c * PB : (c + 1) * PB]


def histories(slips, slot, shift):
    pieces = []
    for b in range(PHASES):
        first = PHASES * shift - b
        low, high = max(first, 0), min(first + PHASES, L)
        if high <= low:
            pieces.append(jnp.zeros((PHASES * V, PB), jnp.bfloat16))
            continue
        parts = [slips[slot, low * V : high * V, :]]
        if low > first:
            parts.insert(0, jnp.zeros(((low - first) * V, PB), jnp.bfloat16))
        if high < first + PHASES:
            parts.append(jnp.zeros(((first + PHASES - high) * V, PB), jnp.bfloat16))
        pieces.append(parts[0] if len(parts) == 1 else jnp.concatenate(parts, axis=0))
    return jnp.concatenate(pieces, axis=1)


def convolve_kernel(arrivals, begins, info_ref, *rest):
    count = len(arrivals)
    tensors, slips, rest = rest[:count], rest[count], rest[count + 1 :]
    before = None
    if not begins:
        before, rest = rest[0], rest[1:]
    out_ref, phases = rest
    for half in range(2):
        phases[half, :, :PADROWS, :] = jnp.zeros((2, PADROWS, PHASES * PB), jnp.float32)
    for n in range(count):
        half = n % 2
        slot = info_ref[arrivals[n]]
        gather_phases(info_ref[SLOTS + arrivals[n]], tensors[n], phases.at[half])
        for c in range(2):
            rows = slice(c * BLOCK, (c + 1) * BLOCK)
            term = None
            for j in range(TAPS):
                shifted = phases[half, c, PADROWS - j : PADROWS - j + BLOCK, :]
                product = lax.dot_general(
                    shifted.astype(jnp.bfloat16),
                    histories(slips, slot, j),
                    (((1,), (1,)), ((), ())),
                    preferred_element_type=jnp.float32,
                )
                term = product if term is None else term + product
            if n > 0:
                out_ref[rows, :] += term
            elif begins:
                out_ref[rows, :] = term
            else:
                out_ref[rows, :] = before[rows, :] + term


def convolve(arrivals, info, tensors, slips, before):
    count = len(arrivals)
    vmem = pl.BlockSpec(memory_space=pltpu.VMEM)
    begins = before is None
    return pl.pallas_call(
        functools.partial(convolve_kernel, arrivals, begins),
        out_shape=jax.ShapeDtypeStruct((2 * BLOCK, PHASES * V), jnp.float32),
        in_specs=[pl.BlockSpec(memory_space=pltpu.SMEM)]
        + [vmem] * (count + 1)
        + ([] if begins else [vmem]),
        out_specs=vmem,
        scratch_shapes=[
            pltpu.VMEM((2, 2, PADROWS + BLOCK, PHASES * PB), jnp.float32),
        ],
        compiler_params=pltpu.CompilerParams(vmem_limit_bytes=LARGE),
        cost_estimate=pl.CostEstimate(
            flops=count * 1800000000, bytes_accessed=count * 1048576, transcendentals=0
        ),
        name="convolve",
    )(info, *tensors, slips, *([] if begins else [before]))


def pick_phases(delay):
    rows = lax.broadcasted_iota(jnp.int32, (BLOCK, 2 * BLOCK), 0)
    lane = lax.broadcasted_iota(jnp.int32, (BLOCK, 2 * BLOCK), 1)
    source = BLOCK + ((rows & 63) << 2) + (rows >> 6) - delay
    return jnp.where(lane == source, 1.0, 0.0).astype(jnp.bfloat16)


def gather_some(delay, blocks, chunks, phases):
    pick = pick_phases(delay)
    part = BLOCK // PHASES
    dims = (((1,), (1,)), ((), ()))
    for place, a in enumerate(chunks):
        moved = lax.dot_general(
            pick[:, BLOCK:], blocks[a], dims, preferred_element_type=jnp.float32
        )
        if a > 0:
            moved += lax.dot_general(
                pick[:, :BLOCK], blocks[a - 1], dims, preferred_element_type=jnp.float32
            )
        low = PADROWS + place * part
        for c in range(2):
            for b in range(PHASES):
                phases[c, low : low + part, b * PB : (b + 1) * PB] = moved[
                    b * part : (b + 1) * part, c * PB : (c + 1) * PB
                ]


def finish_kernel(late, info_ref, place_ref, *rest):
    count = 4 if late else 2
    tensors, rest = rest[:count], rest[count:]
    slips, before, table_ref, weights_ref = rest[:4]
    rest = rest[4:]
    known, peaks = None, None
    if late:
        known, peaks = rest[:2]
        rest = rest[2:]
    out_ref, traces = rest[0], rest[1]
    phases, total, stacked = rest[2:]
    rows = BLOCK // 2
    wide = 2 * V
    first_row = PADROWS + (64 if late else 0)
    if not late:
        phases[:, :, :PADROWS, :] = jnp.zeros((2, 2, PADROWS, PHASES * PB), jnp.float32)
    for n in range(2):
        arrival = SLOTS - 2 + n
        slot = info_ref[arrival]
        halves = tensors[2 * n : 2 * n + 2] if late else tensors[n : n + 1]
        blocks = [half[:, i * BLOCK : (i + 1) * BLOCK] for half in halves for i in range(2)]
        chunks = (1, 2, 3) if late else (0, 1)
        gather_some(info_ref[SLOTS + arrival], blocks, chunks, phases.at[n])
        term = None
        for j in range(TAPS):
            shifted = jnp.concatenate(
                [phases[n, c, first_row - j : first_row - j + rows, :] for c in range(2)], axis=0
            )
            product = lax.dot_general(
                shifted.astype(jnp.bfloat16),
                histories(slips, slot, j),
                (((1,), (1,)), ((), ())),
                preferred_element_type=jnp.float32,
            )
            term = product if term is None else term + product
        if n == 0:
            for c in range(2):
                low = c * BLOCK + (rows if late else 0)
                total[c * rows : (c + 1) * rows, :] = (
                    before[low : low + rows, :] + term[c * rows : (c + 1) * rows, :]
                )
        else:
            total[...] += term

    part = SPAN // PHASES
    spans = rows // part
    lane = lax.broadcasted_iota(jnp.int32, (part, wide), 1)
    for a in range(spans):
        for b in range(PHASES):
            half = slice((b // 2) * wide, (b // 2 + 1) * wide)
            first = total[a * part : (a + 1) * part, half]
            second = total[rows + a * part : rows + (a + 1) * part, half]
            if b % 2 == 0:
                second = pltpu.roll(second, V, 1)
            else:
                first = pltpu.roll(first, V, 1)
            traces[b * part : (b + 1) * part, a * wide : (a + 1) * wide] = jnp.where(
                lane < V, first, second
            ).astype(jnp.bfloat16)

    width = spans * wide
    nothing = jnp.zeros((SPAN, width), jnp.bfloat16)
    stacked[:SPAN, :] = traces[...]
    stacked[SPAN : 2 * SPAN, wide:] = traces[:, : width - wide]
    if late:
        stacked[SPAN : 2 * SPAN, :wide] = known[:, width - wide :]
        stacked[2 * SPAN : 3 * SPAN, :] = known[...]
        near = jnp.concatenate([known[:, 2 * wide :], traces[:, : 2 * wide]], axis=1)
        far = jnp.concatenate([known[:, wide:], traces[:, :wide]], axis=1)
        low = 0
    else:
        stacked[SPAN : 2 * SPAN, :wide] = nothing[:, :wide]
        stacked[2 * SPAN : 3 * SPAN, :] = nothing
        stacked[3 * SPAN :, : 2 * wide] = nothing[:, : 2 * wide]
        near = traces[:, : 2 * wide]
        far = jnp.concatenate([nothing[:, :wide], traces[:, :wide]], axis=1)
        low = 2 * wide
    states = jnp.dot(
        weights_ref[...],
        jnp.concatenate([near, far], axis=0),
        preferred_element_type=jnp.float32,
    )
    stacked[3 * SPAN :, low:] = states.astype(jnp.bfloat16)
    out_ref[...] = peaks[...] if late else jnp.zeros_like(out_ref)

    @pl.loop(0, NPER // QSTEP)
    def _(step):
        table = table_ref[pl.ds(step * QSTEP, QSTEP)].reshape(QSTEP * SPAN, 4 * SPAN)
        deep = 4 * SPAN if late else 2 * SPAN
        one = jnp.dot(
            table[:, :deep], stacked[:deep, : 2 * wide], preferred_element_type=jnp.float32
        )
        two = jnp.dot(table, stacked[:, 2 * wide :], preferred_element_type=jnp.float32)
        both = jnp.maximum(jnp.abs(one), jnp.abs(two))
        for n in range(QSTEP):
            highest = jnp.max(both[n * SPAN : (n + 1) * SPAN], axis=0, keepdims=True)
            highest = jnp.maximum(highest[:, :wide], highest[:, wide:])
            q = step * QSTEP + n
            owner, rank = place_ref[q], place_ref[NPER + q]
            if late:
                highest = jnp.maximum(highest, peaks[owner, pl.ds(rank, 1), :])
            out_ref[owner, pl.ds(rank, 1), :] = highest


def finish(late, info, place, tensors, slips, before, table, weights, known):
    smem = pl.BlockSpec(memory_space=pltpu.SMEM)
    vmem = pl.BlockSpec(memory_space=pltpu.VMEM)
    operands = [*tensors, slips, before, table, weights, *known]
    out_shape = [jax.ShapeDtypeStruct((OWNERS, PMAX, 2 * V), jnp.float32)]
    traces = (SPAN, HALF // SPAN * 2 * V)
    scratch = []
    if late:
        scratch = [pltpu.VMEM(traces, jnp.bfloat16)]
    else:
        out_shape.append(jax.ShapeDtypeStruct(traces, jnp.bfloat16))
    held = PADROWS + (192 if late else 128)
    return pl.pallas_call(
        functools.partial(finish_kernel, late),
        out_shape=out_shape,
        in_specs=[smem, smem] + [vmem] * len(operands),
        out_specs=[vmem] * len(out_shape),
        scratch_shapes=scratch
        + [
            pltpu.VMEM((2, 2, held, PHASES * PB), jnp.float32),
            pltpu.VMEM((BLOCK, PHASES * V), jnp.float32),
            pltpu.VMEM((4 * SPAN, HALF // SPAN * 2 * V), jnp.bfloat16),
        ],
        compiler_params=pltpu.CompilerParams(vmem_limit_bytes=LARGE),
        cost_estimate=pl.CostEstimate(
            flops=3600000000, bytes_accessed=8000000, transcendentals=0
        ),
        name="finish",
    )(info, place, *operands)


def send(block, n):
    pairs = [(g, target(g, *STEPS[n])) for g in range(SLOTS)]
    return lax.ppermute(block, "sgt", pairs)


def local(
    sgt_tensor, moment, slip_rate, footprint, live_blocks, start_delay, frequency, period_owner
):
    here = lax.axis_index("sgt")
    rupture = here * OWNERS + lax.axis_index("work")
    outgoing = list(project(STEPS, footprint, sgt_tensor, moment))
    tensors = [outgoing[0]]
    for n in range(1, SLOTS - 2):
        tensors.append(send(outgoing[n], n))
    first, second = SLOTS - 2, SLOTS - 1
    halves = {first: [], second: []}

    def send_after(part, n, arrived):
        block, tensors[arrived] = lax.optimization_barrier((outgoing[part], tensors[arrived]))
        halves[n].append(send(block, n))

    send_after(SLOTS - 2, first, 1)
    send_after(SLOTS, second, 2)
    slip_rate, frequency, tensors[1] = lax.optimization_barrier(
        (slip_rate, frequency, tensors[1])
    )
    own_blocks = lax.dynamic_index_in_dim(footprint, rupture, 0, keepdims=False)
    own_count = lax.dynamic_index_in_dim(live_blocks, rupture, 0, keepdims=False)
    own_delays = lax.dynamic_index_in_dim(start_delay, rupture, 0, keepdims=False)
    origins = jnp.stack([origin(here, dz, dc) for dz, dc in STEPS])
    match = (own_blocks >> 2)[None, :] == origins[:, None]
    slot = jnp.sum(jnp.where(match, jnp.arange(SLOTS)[None, :], 0), axis=1)
    delay = jnp.sum(jnp.where(match, own_delays[None, :], 0), axis=1)
    info = jnp.concatenate([slot, jnp.where(slot < own_count, delay, 4 * NT)])

    slips = jnp.transpose(slip_rate[0], (0, 3, 1, 2)).reshape(SLOTS, L * V, PB)
    table, weights = tables(frequency)
    period_ids = jnp.arange(NPER)
    same_owner = period_owner[:, None] == period_owner[None, :]
    earlier = period_ids[None, :] < period_ids[:, None]
    rank = jnp.sum(same_owner & earlier, axis=1).astype(jnp.int32)
    place = jnp.concatenate([period_owner, rank])

    running = None
    for n, arrivals in enumerate(GROUPS):
        running = convolve(arrivals, info, [tensors[n] for n in arrivals], slips, running)
        if n == 1:
            outgoing[SLOTS - 1], outgoing[SLOTS + 1], running, table = lax.optimization_barrier(
                (outgoing[SLOTS - 1], outgoing[SLOTS + 1], running, table)
            )
            send_after(SLOTS - 1, first, 4)
            send_after(SLOTS + 1, second, 5)
    peaks, known = finish(
        False,
        info,
        place,
        [halves[first][0], halves[second][0]],
        slips,
        running,
        table,
        weights,
        [],
    )
    (peaks,) = finish(
        True,
        info,
        place,
        halves[first] + halves[second],
        slips,
        running,
        table,
        weights,
        [known, peaks],
    )
    peaks = lax.all_to_all(peaks, "work", split_axis=0, concat_axis=0, tiled=True)
    result = jnp.transpose(peaks.reshape(OWNERS, PMAX, 2, V), (1, 2, 0, 3))
    return result[None]


def solution(mesh):
    in_specs = (
        P("sgt", None, None, None, None),
        P("sgt", None, None),
        P(("sgt", "work"), None, None, None, None),
        P(),
        P(),
        P(),
        P(),
        P(),
    )
    out_specs = P("work", None, None, "sgt", None)
    return jax.shard_map(local, mesh=mesh, in_specs=in_specs, out_specs=out_specs, check_vma=False)
```
